128 devices in a mesh: col: 32 (over y, x, core), row: 4 (over z).
Axes of the slice: x: 4, y: 4, z: 4, core: 2. Of those that a mesh axis runs over, the one named last changes fastest.
Arguments:
- base_rhs: float32 [256, 512, 128], P(('col', 'row')), may hold values from -6 to 6
- base_inverse: bfloat16 [256, 512, 512], P(('col', 'row')), may hold values from -0.5 to 1.2, as said below
- apex_righthand_vectors: float32 [5, 4, 512, 128], P(None, 'row'), may hold values from -6 to 6
- top_inverse: bfloat16 [5, 4, 512, 512], P(None, 'row'), may hold values from -0.5 to 1.2, as said below
- factor_blocks: bfloat16 [5, 768, 512, 512], P(None, ('col', 'row')), may hold values from -0.06187184 to 0.06187184
- block_source: int32 [5, 768], P(None, ('col', 'row')), may hold values from 0 to 23, as said below
- block_count: int32 [5, 128], P(None, ('col', 'row')), may hold values from 1 to 6, as said below
Outputs:
- base_solution: float32 [256, 512, 128], P(('col', 'row'))
- top_solution: float32 [5, 4, 512, 128], P(None, 'row')
The draws below stay inside these ranges and needn't reach their ends.
Inputs may be any that keep to these rules, and one draw needn't show every extreme that they name: `base_inverse`: lower triangular; diagonal entries between 0.6 and 1.2. `top_inverse`: lower triangular; diagonal entries between 0.6 and 1.2. `block_source`: the first block_count entries of a list are strictly increasing. An entry below 8 names a base supernode of the device's process column; an entry q above names the top supernode of level u = (q - 8) // 4, lower than the list's level, and stands only on devices of process column u mod 32. The other entries are 0. `block_count`: every top level has a device with 6 live slots.
All inputs are finite; a program needn't handle non-finite values.
Results may differ from the reference program's by a relative error of at most 0.0075.
Values may be sent and summed in bfloat16 or wider, within the bound.
No kernel may reach another device: no remote copies, remote signals or barrier semaphores. Data moves between devices by JAX's collectives and lax.ppermute only.
A program may use at most 128 MiB of HBM per device.

```python
import math
import jax
import jax.numpy as jnp
from jax import lax

B = 512
R = 128
SB = 2
NBLK = 6
TOP = 5
N_COL = 32
N_ROW = 4
DEVICES = 128


def triangular(key, array_shape):
    key_below, key_diag = jax.random.split(key)
    spread_factor = 0.5 / math.sqrt(B)
    below_part = jnp.clip(jax.random.normal(key_below, array_shape, jnp.float32), -3.0, 3.0) * spread_factor
    diagonal = 0.6 + 0.59 * jax.random.uniform(key_diag, array_shape, jnp.float32)
    beneath_number = lax.broadcasted_iota(jnp.int32, array_shape, len(array_shape) - 2)
    upper_index = lax.broadcasted_iota(jnp.int32, array_shape, len(array_shape) - 1)
    return jnp.where(upper_index < beneath_number, below_part, jnp.where(upper_index == beneath_number, diagonal, jnp.float32(0.0)))


def draw_base_inverse(key, part):
    return triangular(jax.random.fold_in(key, 1), (DEVICES * SB, B, B)).astype(jnp.bfloat16)


def draw_top_inverse(key, part):
    return triangular(jax.random.fold_in(key, 2), (TOP, N_ROW, B, B)).astype(jnp.bfloat16)


def make_lists(key):
    key_full, key_pick, key_small, key_rank, key_last = jax.random.split(jax.random.fold_in(key, 7), 5)
    full_rows = jax.random.randint(key_full, (TOP, DEVICES), 0, 8) == 0
    picked_any = jax.random.randint(key_pick, (TOP, 1), 0, DEVICES)
    picked_last = (TOP - 2) % N_COL * N_ROW + jax.random.randint(key_last, (TOP, 1), 0, N_ROW)
    level_rows = lax.broadcasted_iota(jnp.int32, (TOP, 1), 0)
    picked = jnp.where(level_rows == TOP - 1, picked_last, picked_any)
    device_index = lax.broadcasted_iota(jnp.int32, (TOP, DEVICES), 1)
    full_rows = full_rows | (device_index == picked)
    small_count = jnp.minimum(jax.random.randint(key_small, (TOP, DEVICES), 1, 4), NBLK)
    counts = jnp.where(full_rows, NBLK, small_count).astype(jnp.int32)
    reference_aggregate = N_ROW * SB
    trial_aggregate = reference_aggregate + (TOP - 1) * N_ROW
    grid_shape = (TOP, DEVICES, trial_aggregate)
    trial_slot_number = lax.broadcasted_iota(jnp.int32, grid_shape, 2)
    level_index = lax.broadcasted_iota(jnp.int32, grid_shape, 0)
    column_position_index = lax.broadcasted_iota(jnp.int32, grid_shape, 1) // N_ROW
    top_level = (trial_slot_number - reference_aggregate) // N_ROW
    allowed = (trial_slot_number < reference_aggregate) | (top_level < level_index) & (top_level % N_COL == column_position_index)
    random_rank = jax.random.randint(key_rank, grid_shape, 0, 4096)
    process_sequence = random_rank * trial_aggregate + trial_slot_number
    higher_tier_reward = 4096 * trial_aggregate
    process_sequence = jnp.where(trial_slot_number >= reference_aggregate, process_sequence + higher_tier_reward, process_sequence)
    process_sequence = jnp.where(allowed, process_sequence, -1)
    ranked_values, chosen = lax.top_k(process_sequence, NBLK)
    slot_index = lax.broadcasted_iota(jnp.int32, (TOP, DEVICES, NBLK), 2)
    live_slots = slot_index < counts[:, :, None]
    ordered = jnp.sort(jnp.where(live_slots, chosen, trial_aggregate), axis=-1)
    sources = jnp.where(live_slots, ordered, 0).astype(jnp.int32)
    return (sources.reshape(TOP, DEVICES * NBLK), counts)


def draw_block_source(key, part):
    return make_lists(key)[0]


def draw_block_count(key, part):
    return make_lists(key)[1]


def draw_factor_blocks(key, part):
    sources, counts = make_lists(key)
    group_count = TOP * DEVICES
    slot_number = lax.broadcasted_iota(jnp.int32, (group_count, NBLK), 1)
    live_slots = slot_number < counts.reshape(group_count, 1)
    top_slots = live_slots & (sources.reshape(group_count, NBLK) >= N_ROW * SB)
    base_scale = 1.0 / math.sqrt(3 * B * N_COL)
    top_scale = 0.35 / math.sqrt(B)
    slot_scales = jnp.where(top_slots, jnp.float32(top_scale), jnp.float32(base_scale))
    block_key = jax.random.fold_in(key, 3)
    group_numbers = jnp.arange(group_count, dtype=jnp.int32)

    def one_group(payload):
        group_number, group_scales = payload
        group_key = jax.random.fold_in(block_key, group_number)
        block_shape = (NBLK, B, B)
        values = jnp.clip(jax.random.normal(group_key, block_shape, jnp.float32), -4.0, 4.0)
        return (values * group_scales[:, None, None]).astype(jnp.bfloat16)
    blocks = lax.map(one_group, (group_numbers, slot_scales))
    return blocks.reshape(TOP, DEVICES * NBLK, B, B)


def steps_of(stream_key, dims, pieces, low, largest):
    def one(dim, shards_of):
        steps = jax.random.uniform(jax.random.fold_in(jax.random.fold_in(stream_key, 6), dim), (shards_of,), jnp.float32, low / len(pieces), largest / len(pieces))
        return jnp.repeat(jnp.exp(steps), dims[dim] // shards_of).reshape((-1,) + (1,) * (len(dims) - dim - 1))

    factor_of = one(*pieces[0])
    for cut in pieces[1:]:
        factor_of = factor_of * one(*cut)
    return factor_of


def noise(stream_key, extent, scale, bound, shards=(), held_as=jnp.bfloat16):
    factor_of = steps_of(stream_key, extent, shards, -0.22, 0.18) if shards else 1.0
    drawn = jax.random.normal(stream_key, extent, jnp.float32) * scale * factor_of
    return jnp.minimum(jnp.maximum(drawn, -bound), bound).astype(held_as)


def setup_inputs(seed: int = 0) -> dict:
    key_list = jax.random.split(jax.random.key(seed), 8)
    base_rhs = noise(key_list[0], (DEVICES * SB, B, R), 1.0, 6.0, ((0, 128),), jnp.float32)
    base_inverse = draw_base_inverse(jax.random.fold_in(key_list[7], 71), 0)
    apex_righthand_vectors = noise(key_list[2], (TOP, N_ROW, B, R), 1.0, 6.0, ((1, 4),), jnp.float32)
    top_inverse = draw_top_inverse(jax.random.fold_in(key_list[7], 71), 0)
    factor_blocks = draw_factor_blocks(jax.random.fold_in(key_list[7], 71), 0)
    block_source = draw_block_source(jax.random.fold_in(key_list[7], 71), 0)
    block_count = draw_block_count(jax.random.fold_in(key_list[7], 71), 0)
    return {"base_rhs": base_rhs, "base_inverse": base_inverse, "apex_righthand_vectors": apex_righthand_vectors, "top_inverse": top_inverse, "factor_blocks": factor_blocks, "block_source": block_source, "block_count": block_count}


def solve_blocks(inverses, rights):
    def one_block(pair):
        return jnp.dot(pair[0], pair[1].astype(jnp.bfloat16), preferred_element_type=jnp.float32)
    return lax.map(one_block, (inverses, rights))


def reference(base_rhs, base_inverse, apex_righthand_vectors, top_inverse, factor_blocks, block_source, block_count):
    base_solution = solve_blocks(base_inverse, base_rhs)
    bottom_quantized = base_solution.astype(jnp.bfloat16)
    reference_aggregate = N_ROW * SB
    column_of = jnp.arange(N_COL * N_ROW, dtype=jnp.int32) // N_ROW
    slot_index = jnp.arange(NBLK, dtype=jnp.int32)
    table = bottom_quantized
    solutions = []
    for level_index in range(TOP):
        blocks = factor_blocks[level_index].reshape(N_COL * N_ROW, NBLK, B, B)
        picks = block_source[level_index].reshape(N_COL * N_ROW, NBLK)
        rows_of = jnp.where(picks < reference_aggregate, column_of[:, None] * reference_aggregate + picks,
                            N_COL * N_ROW * SB + picks - reference_aggregate).astype(jnp.int32)
        current = table

        def device_partial(item):
            block_group, row_group, live_count = item
            live_slots = slot_index < live_count
            masked = jnp.where(live_slots[:, None, None], block_group.astype(jnp.float32), jnp.float32(0.0))
            operands = jnp.take(current, row_group, axis=0).astype(jnp.float32)
            return jnp.einsum("sij,sjr->ir", masked, operands, precision=lax.Precision.HIGHEST)

        partials = lax.map(device_partial, (blocks, rows_of, block_count[level_index]))
        level_sum = jnp.sum(partials.reshape(N_COL, N_ROW, B, R), axis=0)
        correction = (apex_righthand_vectors[level_index] - level_sum).astype(jnp.bfloat16)
        top_solution = solve_blocks(top_inverse[level_index], correction)
        solutions.append(top_solution)
        table = jnp.concatenate([table, top_solution.astype(jnp.bfloat16)], axis=0)
    return base_solution, jnp.stack(solutions)
```

```python
import functools

import jax
import jax.numpy as jnp
from jax import lax
from jax.experimental import pallas as pl
from jax.experimental.pallas import tpu as pltpu
from jax.sharding import PartitionSpec as P

BF16, F32 = jnp.bfloat16, jnp.float32
AXES = ("col", "row")
NX = NY = NZ = 4
BOTH = (0, 1)
ANY = pl.BlockSpec(memory_space=pl.ANY)
SMEM = pl.BlockSpec(memory_space=pltpu.SMEM)
VMEM = pl.BlockSpec(memory_space=pltpu.VMEM)


def column(x, y, core):
    return (y * NX + x) * 2 + core


def place(x, y, core, z):
    return column(x, y, core) * NZ + z


def dot(a, b):
    return jnp.dot(a, b, preferred_element_type=F32)


def params():
    return pltpu.CompilerParams(vmem_limit_bytes=48 * 1024 * 1024)


def live(source_ref, count_ref, level, slot, low, high):
    source = source_ref[level, slot]
    return (slot < count_ref[level, 0]) & (source >= low) & (source < high)


def block_copy(factor_ref, held, sems, level, slot, index):
    return pltpu.make_async_copy(factor_ref.at[level, slot], held.at[index], sems.at[index])


def products(levels, slots, low, high, row, source_ref, count_ref, factor_ref, piece_refs, per_row,
             held, operands, total, sems, piece_sems):
    for i, level in enumerate(levels):
        for slot in range(slots):
            @pl.when(live(source_ref, count_ref, level, slot, low, high))
            def _():
                block_copy(factor_ref, held, sems, level, slot, i * slots + slot).start()
    piece_copies = []
    for k, piece in enumerate(piece_refs):
        owner = lax.rem(row + NZ - k, NZ)
        copy = pltpu.make_async_copy(piece, operands.at[owner], piece_sems.at[k])
        copy.start()
        piece_copies.append(copy)
    total[...] = jnp.zeros_like(total)
    for copy in piece_copies:
        copy.wait()
    for i, level in enumerate(levels):
        for slot in range(slots):
            @pl.when(live(source_ref, count_ref, level, slot, low, high))
            def _():
                block_copy(factor_ref, held, sems, level, slot, i * slots + slot).wait()
                q = source_ref[level, slot] - low
                if per_row == 1:
                    operand = operands[q]
                else:
                    operand = operands[q // per_row, q % per_row]
                total[i] += dot(held[i * slots + slot], operand)


def base_kernel(levels, slots, place_ref, source_ref, count_ref, factor_ref, *rest):
    pieces, (keep_ref, send_ref), scratch = rest[:NZ], rest[NZ : NZ + 2], rest[NZ + 2 :]
    row, core = place_ref[0], place_ref[1]
    held, operands, total, sems, piece_sems = scratch
    per_row = operands.shape[1]
    products(range(levels), slots, 0, NZ * per_row, row, source_ref, count_ref, factor_ref, pieces, per_row,
             held, operands, total, sems, piece_sems)
    for i, (on_first, on_second) in enumerate(((0, 0), (1, 2), (3, 4))):
        keep_ref[i] = total[jnp.where(core == 0, on_first, on_second)]
        send_ref[i] = total[jnp.where(core == 0, on_second, on_first)].astype(BF16)


def solve_kernel(level, slots, low, place_ref, source_ref, count_ref, factor_ref, ahead_ref, inverse_ref, *rest):
    pieces, (out_ref,), scratch = rest[:NZ], rest[NZ : NZ + 1], rest[NZ + 1 :]
    held, operands, total, sems, piece_sems = scratch
    products((level,), slots, low, low + NZ, place_ref[0], source_ref, count_ref, factor_ref, pieces, 1,
             held, operands, total, sems, piece_sems)
    correction = (ahead_ref[...] - total[0]).astype(BF16)
    out_ref[...] = dot(inverse_ref[...], correction).astype(BF16)


def later_kernel(levels, slots, low, place_ref, source_ref, count_ref, factor_ref, *rest):
    pieces, (out_ref,), scratch = rest[:NZ], rest[NZ : NZ + 1], rest[NZ + 1 :]
    held, operands, total, sems, piece_sems = scratch
    products(levels, slots, low, low + NZ, place_ref[0], source_ref, count_ref, factor_ref, pieces, 1,
             held, operands, total, sems, piece_sems)
    out_ref[...] = total[...].astype(BF16)


def scratch(levels, slots, block, per_row, dtype_rows):
    shape = (NZ,) + ((per_row,) if per_row > 1 else ()) + dtype_rows
    return [
        pltpu.VMEM((levels * slots,) + block, BF16),
        pltpu.VMEM(shape, BF16),
        pltpu.VMEM((levels,) + dtype_rows, F32),
        pltpu.SemaphoreType.DMA((levels * slots,)),
        pltpu.SemaphoreType.DMA((NZ,)),
    ]


def send(value, pairs):
    return lax.ppermute(value, AXES, pairs)


def to_row_offset(sender, receiver, k):
    return [(sender * NZ + v, receiver * NZ + (v + k) % NZ) for v in range(NZ)]


def sum_to_root(value, root_x, cores):
    sent = value.astype(BF16)
    for dx in (1, 3, 2):
        value = value + send(sent, [
            (place((root_x + dx) % NX, y, core, z), place(root_x, y, core, z))
            for y in range(NY) for core in cores for z in range(NZ)
        ]).astype(F32)
    sent = value.astype(BF16)
    for y in (1, 3, 2):
        value = value + send(sent, [
            (place(root_x, y, core, z), place(root_x, 0, core, z)) for core in cores for z in range(NZ)
        ]).astype(F32)
    return value


def spread(value, x0, core, here):
    value = jnp.where(here == column(x0, 0, core), value, jnp.zeros_like(value))
    first = value
    for dx in (1, 3, 2):
        value = value + send(first, [(place(x0, 0, core, z), place((x0 + dx) % NX, 0, core, z)) for z in range(NZ)])
    first = value
    for y in (1, 3, 2):
        value = value + send(first, [
            (place(x, 0, core, z), place(x, y, core, z)) for x in range(NX) for z in range(NZ)
        ])
    return value + send(value, [
        (place(x, y, core, z), place(x, y, 1 - core, z)) for x in range(NX) for y in range(NY) for z in range(NZ)
    ])


def on_device(base_rhs, base_inverse, apex, top_inverse, factor_blocks, block_source, block_count):
    levels, slots = block_source.shape[0], factor_blocks.shape[1]
    per_row, size, samples = base_rhs.shape
    block = factor_blocks.shape[2:]
    here, row = lax.axis_index("col"), lax.axis_index("row")
    core = here % 2
    places = jnp.stack([row, core]).astype(jnp.int32)

    base_solution = jnp.einsum("sij,sjr->sir", base_inverse, base_rhs.astype(BF16), preferred_element_type=F32)
    rounded = base_solution.astype(BF16)
    pieces = [rounded] + [
        lax.ppermute(rounded, "row", [(z, (z + k) % NZ) for z in range(NZ)]) for k in (1, 2, 3)
    ]
    keep, give = pl.pallas_call(
        functools.partial(base_kernel, levels, slots),
        out_shape=(
            jax.ShapeDtypeStruct((3, size, samples), F32),
            jax.ShapeDtypeStruct((3, size, samples), BF16),
        ),
        in_specs=[SMEM, SMEM, SMEM, ANY] + [ANY] * NZ,
        out_specs=(VMEM, VMEM),
        scratch_shapes=scratch(levels, slots, block, per_row, (size, samples)),
        compiler_params=params(),
        name="base_products",
    )(places, block_source, block_count, factor_blocks, *pieces)
    got = lax.ppermute(give, "col", [(c, c ^ 1) for c in range(NX * NY * 2)])
    pair = keep + got.astype(F32)
    sums = [sum_to_root(pair[0], 0, (0,)), sum_to_root(pair[1], 0, BOTH), sum_to_root(pair[2], 1, BOTH)]
    sum_of = [sums[0], sums[1], sums[1], sums[2], sums[2]]
    ahead = [apex[t, 0] - sum_of[t] for t in range(levels)]

    first = dot(top_inverse[0, 0], ahead[0].astype(BF16)).astype(BF16)
    solved = [first]
    for u in range(levels - 1):
        sender = max(u - 1, 0)
        pieces = [
            solved[u] if sender == u and k == 0 else send(solved[u], to_row_offset(sender, u, k)) for k in range(NZ)
        ]
        common = (places, block_source, block_count, factor_blocks)
        low = per_row * NZ + u * NZ
        solved.append(
            pl.pallas_call(
                functools.partial(solve_kernel, u + 1, slots, low),
                out_shape=jax.ShapeDtypeStruct((size, samples), BF16),
                in_specs=[SMEM, SMEM, SMEM, ANY, VMEM, VMEM] + [ANY] * NZ,
                out_specs=VMEM,
                scratch_shapes=scratch(1, slots, block, 1, (size, samples)),
                compiler_params=params(),
                name=f"solve_{u + 1}",
            )(*common, ahead[u + 1], top_inverse[u + 1, 0], *pieces)
        )
        later = tuple(range(u + 2, levels))
        if later:
            made = pl.pallas_call(
                functools.partial(later_kernel, later, slots, low),
                out_shape=jax.ShapeDtypeStruct((len(later), size, samples), BF16),
                in_specs=[SMEM, SMEM, SMEM, ANY] + [ANY] * NZ,
                out_specs=VMEM,
                scratch_shapes=scratch(len(later), slots, block, 1, (size, samples)),
                compiler_params=params(),
                name=f"later_{u}",
            )(*common, *pieces)
            for i, t in enumerate(later):
                arrived = send(made[i], to_row_offset(u, t - 1, 0))
                ahead[t] = ahead[t] - arrived.astype(F32)
    out = [spread(jnp.stack(solved[:2]), 0, 0, here)]
    out += [spread(solved[t][None], (t - 1) // 2, (t - 1) % 2, here) for t in range(2, levels)]
    return base_solution, jnp.concatenate(out).astype(F32)[:, None]


def solution(mesh):
    placed = (
        P(AXES, None, None),
        P(AXES, None, None),
        P(None, "row", None, None),
        P(None, "row", None, None),
        P(None, AXES, None, None),
        P(None, AXES),
        P(None, AXES),
    )
    return jax.shard_map(
        on_device,
        mesh=mesh,
        in_specs=placed,
        out_specs=(P(AXES, None, None), P(None, "row", None, None)),
        check_vma=False,
    )
```

```python
import functools

import jax
import jax.numpy as jnp
from jax import lax
from jax.experimental import pallas as pl
from jax.experimental.pallas import tpu as pltpu
from jax.sharding import PartitionSpec as P

BF16, F32 = jnp.bfloat16, jnp.float32
AXES = ("col", "row")
NX = NY = NZ = 4
BOTH = (0, 1)
CHAIN = 4
ANY = pl.BlockSpec(memory_space=pl.ANY)
SMEM = pl.BlockSpec(memory_space=pltpu.SMEM)
VMEM = pl.BlockSpec(memory_space=pltpu.VMEM)


def column(x, y, core):
    return (y * NX + x) * 2 + core


def place(x, y, core, z):
    return column(x, y, core) * NZ + z


def dot(a, b):
    return jnp.dot(a, b, preferred_element_type=F32)


def params():
    return pltpu.CompilerParams(vmem_limit_bytes=48 * 1024 * 1024)


def live(source_ref, count_ref, level, slot, low, high):
    source = source_ref[level, slot]
    return (slot < count_ref[level, 0]) & (source >= low) & (source < high)


def block_copy(factor_ref, held, sems, level, slot, index):
    return pltpu.make_async_copy(factor_ref.at[level, slot], held.at[index], sems.at[index])


def products(levels, slots, low, high, row, source_ref, count_ref, factor_ref, piece_refs, per_row,
             held, operands, total, sems, piece_sems):
    for i, level in enumerate(levels):
        for slot in range(slots):
            @pl.when(live(source_ref, count_ref, level, slot, low, high))
            def _():
                block_copy(factor_ref, held, sems, level, slot, i * slots + slot).start()
    piece_copies = []
    for k, piece in enumerate(piece_refs):
        owner = lax.rem(row + NZ - k, NZ)
        copy = pltpu.make_async_copy(piece, operands.at[owner], piece_sems.at[k])
        copy.start()
        piece_copies.append(copy)
    total[...] = jnp.zeros_like(total)
    for copy in piece_copies:
        copy.wait()
    for i, level in enumerate(levels):
        for slot in range(slots):
            @pl.when(live(source_ref, count_ref, level, slot, low, high))
            def _():
                block_copy(factor_ref, held, sems, level, slot, i * slots + slot).wait()
                q = source_ref[level, slot] - low
                if per_row == 1:
                    operand = operands[q]
                else:
                    operand = operands[q // per_row, q % per_row]
                total[i] += dot(held[i * slots + slot], operand)


def base_kernel(levels, slots, place_ref, source_ref, count_ref, factor_ref, *rest):
    pieces, (keep_ref, send_ref), scratch = rest[:NZ], rest[NZ : NZ + 2], rest[NZ + 2 :]
    row, core = place_ref[0], place_ref[1]
    held, operands, total, sems, piece_sems = scratch
    per_row = operands.shape[1]
    products(range(levels), slots, 0, NZ * per_row, row, source_ref, count_ref, factor_ref, pieces, per_row,
             held, operands, total, sems, piece_sems)
    shares, some = keep_ref.shape[0], keep_ref.shape[1] // levels
    mine = pl.multiple_of(core * shares * some, shares * some)
    other = pl.multiple_of((1 - core) * shares * some, shares * some)
    for share in range(shares):
        for level in range(levels):
            place_in = pl.ds(level * some, some)
            keep_ref[share, place_in] = total[level, pl.ds(mine + share * some, some)]
            send_ref[share, place_in] = total[level, pl.ds(other + share * some, some)].astype(BF16)


def solve_kernel(level, slots, low, place_ref, source_ref, count_ref, factor_ref, ahead_ref, inverse_ref, *rest):
    pieces, (out_ref,), scratch = rest[:NZ], rest[NZ : NZ + 1], rest[NZ + 1 :]
    held, operands, total, sems, piece_sems = scratch
    products((level,), slots, low, low + NZ, place_ref[0], source_ref, count_ref, factor_ref, pieces, 1,
             held, operands, total, sems, piece_sems)
    correction = (ahead_ref[...] - total[0]).astype(BF16)
    out_ref[...] = dot(inverse_ref[...], correction).astype(BF16)


def later_kernel(levels, slots, low, place_ref, source_ref, count_ref, factor_ref, *rest):
    pieces, (out_ref,), scratch = rest[:NZ], rest[NZ : NZ + 1], rest[NZ + 1 :]
    held, operands, total, sems, piece_sems = scratch
    products(levels, slots, low, low + NZ, place_ref[0], source_ref, count_ref, factor_ref, pieces, 1,
             held, operands, total, sems, piece_sems)
    out_ref[...] = total[...]


def scratch(levels, slots, block, per_row, dtype_rows):
    shape = (NZ,) + ((per_row,) if per_row > 1 else ()) + dtype_rows
    return [
        pltpu.VMEM((levels * slots,) + block, BF16),
        pltpu.VMEM(shape, BF16),
        pltpu.VMEM((levels,) + dtype_rows, F32),
        pltpu.SemaphoreType.DMA((levels * slots,)),
        pltpu.SemaphoreType.DMA((NZ,)),
    ]


def send(value, pairs):
    return lax.ppermute(value, AXES, pairs)


def to_row_offset(sender, receiver, k):
    return [(sender * NZ + v, receiver * NZ + (v + k) % NZ) for v in range(NZ)]


def other_core(value):
    return lax.ppermute(value, "col", [(c, c ^ 1) for c in range(NX * NY * 2)])


def over_plane(value):
    groups = [[column(x, y, core) for y in range(NY) for x in range(NX)] for core in BOTH]
    return lax.all_to_all(value, "col", 0, 0, axis_index_groups=groups, tiled=True)


def spread(value, here):
    x0, core = (CHAIN - 1) // 2, (CHAIN - 1) % 2
    value = jnp.where(here == column(x0, 0, core), value, jnp.zeros_like(value))
    first = value
    for dx in (1, 3, 2):
        value = value + send(first, [(place(x0, 0, core, z), place((x0 + dx) % NX, 0, core, z)) for z in range(NZ)])
    first = value
    for y in (1, 3, 2):
        value = value + send(first, [
            (place(x, 0, core, z), place(x, y, core, z)) for x in range(NX) for z in range(NZ)
        ])
    return value + other_core(value)


def on_device(base_rhs, base_inverse, apex, top_inverse, factor_blocks, block_source, block_count):
    levels, slots = block_source.shape[0], factor_blocks.shape[1]
    per_row, size, samples = base_rhs.shape
    shares = NX * NY
    some = size // 2 // shares
    block = factor_blocks.shape[2:]
    here, row = lax.axis_index("col"), lax.axis_index("row")
    core = here % 2
    places = jnp.stack([row, core]).astype(jnp.int32)
    common = (places, block_source, block_count, factor_blocks)
    after = lax.optimization_barrier

    base_solution = jnp.einsum("sij,sjr->sir", base_inverse, base_rhs.astype(BF16), preferred_element_type=F32)
    rounded = base_solution.astype(BF16)
    pieces = [rounded] + [
        lax.ppermute(rounded, "row", [(z, (z + k) % NZ) for z in range(NZ)]) for k in (1, 2, 3)
    ]
    keep, give = pl.pallas_call(
        functools.partial(base_kernel, levels, slots),
        out_shape=(
            jax.ShapeDtypeStruct((shares, levels * some, samples), F32),
            jax.ShapeDtypeStruct((shares, levels * some, samples), BF16),
        ),
        in_specs=[SMEM, SMEM, SMEM, ANY] + [ANY] * NZ,
        out_specs=(VMEM, VMEM),
        scratch_shapes=scratch(levels, slots, block, per_row, (size, samples)),
        compiler_params=params(),
        name="base_products",
    )(*common, *pieces)
    pair = (keep + other_core(give).astype(F32)).astype(BF16)
    share = jnp.sum(over_plane(pair).astype(F32), axis=0).astype(BF16)
    half = over_plane(jnp.broadcast_to(share[None], (shares,) + share.shape))
    other = other_core(half)
    sums = jnp.where(core == 0, jnp.stack([half, other]), jnp.stack([other, half]))
    sums = sums.reshape(2, shares, levels, some, samples)

    def sum_of(t):
        return sums[:, :, t].reshape(size, samples).astype(F32)

    first = dot(top_inverse[0, 0], (apex[0, 0] - sum_of(0)).astype(BF16)).astype(BF16)
    first, sums = after((first, sums))
    ahead = [apex[t, 0] - sum_of(t) for t in range(levels)]

    solved, kept, moving = [first], [], []
    for u in range(levels - 1):
        sender = max(u - 1, 0)
        pieces = [
            solved[u] if sender == u and k == 0 else send(solved[u], to_row_offset(sender, u, k)) for k in range(NZ)
        ]
        low = per_row * NZ + u * NZ
        target = ahead[u + 1] - moving[0].astype(F32) if u else ahead[u + 1]
        solved.append(
            pl.pallas_call(
                functools.partial(solve_kernel, u + 1, slots, low),
                out_shape=jax.ShapeDtypeStruct((size, samples), BF16),
                in_specs=[SMEM, SMEM, SMEM, ANY, VMEM, VMEM] + [ANY] * NZ,
                out_specs=VMEM,
                scratch_shapes=scratch(1, slots, block, 1, (size, samples)),
                compiler_params=params(),
                name=f"solve_{u + 1}",
            )(*common, target, top_inverse[u + 1, 0], *pieces)
        )
        kept.append(pieces[0])
        later = tuple(range(u + 2, levels))
        if later:
            pieces, solved[-1] = after((pieces, solved[-1]))
            made = pl.pallas_call(
                functools.partial(later_kernel, later, slots, low),
                out_shape=jax.ShapeDtypeStruct((len(later), size, samples), F32),
                in_specs=[SMEM, SMEM, SMEM, ANY] + [ANY] * NZ,
                out_specs=VMEM,
                scratch_shapes=scratch(len(later), slots, block, 1, (size, samples)),
                compiler_params=params(),
                name=f"later_{u}",
            )(*common, *pieces)
            if u:
                made = made + moving[1:].astype(F32)
            moving = send(jnp.concatenate([made.astype(BF16), jnp.stack(kept)]), to_row_offset(u, u + 1, 0))
            moving, kept = moving[: len(later)], [moving[len(later) + i] for i in range(u + 1)]
    old = spread(jnp.stack(kept[:-1]), here)
    out = jnp.concatenate([old, spread(jnp.stack([kept[-1], solved[-1]]), here)])
    return base_solution, out.astype(F32)[:, None]


def solution(mesh):
    placed = (
        P(AXES, None, None),
        P(AXES, None, None),
        P(None, "row", None, None),
        P(None, "row", None, None),
        P(None, AXES, None, None),
        P(None, AXES),
        P(None, AXES),
    )
    return jax.shard_map(
        on_device,
        mesh=mesh,
        in_specs=placed,
        out_specs=(P(AXES, None, None), P(None, "row", None, None)),
        check_vma=False,
    )
```

```python
import functools

import jax
import jax.numpy as jnp
from jax import lax
from jax.experimental import pallas as pl
from jax.experimental.pallas import tpu as pltpu
from jax.sharding import PartitionSpec as P

BF16, F32 = jnp.bfloat16, jnp.float32
AXES = ("col", "row")
NX = NY = NZ = 4
BOTH = (0, 1)
SMEM = pl.BlockSpec(memory_space=pltpu.SMEM)
VMEM = pl.BlockSpec(memory_space=pltpu.VMEM)
ANY = pl.BlockSpec(memory_space=pl.ANY)


def column(x, y, core):
    return (y * NX + x) * 2 + core


def place(x, y, core, z):
    return column(x, y, core) * NZ + z


def dot(a, b):
    return jnp.dot(a, b, preferred_element_type=F32)


def call(body, name, outs, in_specs, args, scratch=(), flops=0, nbytes=0, out_specs=None):
    return pl.pallas_call(
        body,
        out_shape=outs,
        in_specs=in_specs,
        out_specs=out_specs or jax.tree.map(lambda _: VMEM, outs),
        scratch_shapes=list(scratch),
        compiler_params=pltpu.CompilerParams(vmem_limit_bytes=24 * 1024 * 1024),
        cost_estimate=pl.CostEstimate(flops=flops, bytes_accessed=nbytes, transcendentals=0),
        name=name,
    )(*args)


def base_solve_kernel(inverse_ref, rhs_ref, out_ref, rounded_ref):
    for i in range(rhs_ref.shape[0]):
        value = dot(inverse_ref[i], rhs_ref[i].astype(BF16))
        out_ref[i] = value
        rounded_ref[i] = value.astype(BF16)


def load_kernel(levels, slots, count_ref, factor_ref, inverse_ref, held_ref, kept_ref, sems, other_sem):
    inverses = pltpu.make_async_copy(inverse_ref, kept_ref, other_sem)
    inverses.start()

    def each(act):
        for level in range(levels):
            for slot in range(slots):
                @pl.when(slot < count_ref[level, 0])
                def _():
                    at = level * slots + slot
                    act(pltpu.make_async_copy(factor_ref.at[level, slot], held_ref.at[at], sems.at[at]))

    each(lambda copy: copy.start())
    each(lambda copy: copy.wait())
    inverses.wait()


def add_products(total, level, slots, low, high, operand_of, source_ref, count_ref, held_ref):
    for slot in range(slots):
        source = source_ref[level, slot]

        @pl.when((slot < count_ref[level, 0]) & (source >= low) & (source < high))
        def _():
            total[...] += dot(held_ref[level * slots + slot], operand_of(source - low))


def order_pieces(row, piece_refs, operands):
    for k, piece in enumerate(piece_refs):
        operands[lax.rem(row + NZ - k, NZ)] = piece[...]


def base_kernel(levels, slots, place_ref, source_ref, count_ref, held_ref, *rest):
    pieces, (keep_ref, send_ref), (operands, total) = rest[:NZ], rest[NZ : NZ + 2], rest[NZ + 2 :]
    core, per_row = place_ref[1], operands.shape[1]
    order_pieces(place_ref[0], pieces, operands)
    shares, some = keep_ref.shape[0], keep_ref.shape[1] // levels
    mine = pl.multiple_of(core * shares * some, shares * some)
    other = pl.multiple_of((1 - core) * shares * some, shares * some)
    for level in range(levels):
        total[...] = jnp.zeros_like(total)
        add_products(total, level, slots, 0, NZ * per_row, lambda q: operands[q // per_row, lax.rem(q, per_row)],
                     source_ref, count_ref, held_ref)
        for share in range(shares):
            place_in = pl.ds(level * some, some)
            keep_ref[share, place_in] = total[pl.ds(mine + share * some, some)]
            send_ref[share, place_in] = total[pl.ds(other + share * some, some)].astype(BF16)


def first_kernel(place_ref, half_ref, other_ref, apex_ref, inverse_ref, ahead_ref, out_ref, target):
    core = place_ref[1]
    levels = apex_ref.shape[0]
    shares, some = half_ref.shape[0], half_ref.shape[1] // levels
    for level in range(levels):
        to = target if level == 0 else ahead_ref.at[level - 1]
        for ref, side in ((half_ref, core), (other_ref, 1 - core)):
            for share in range(shares):
                rows = pl.ds(pl.multiple_of(side * shares * some, shares * some) + share * some, some)
                to[rows] = apex_ref[level, rows] - ref[share, pl.ds(level * some, some)].astype(F32)
        if level == 0:
            out_ref[...] = dot(inverse_ref[0], target[...].astype(BF16)).astype(BF16)


def sum_kernel(in_ref, out_ref):
    total = in_ref[0].astype(F32)
    for i in range(1, in_ref.shape[0]):
        total = total + in_ref[i].astype(F32)
    for i in range(in_ref.shape[0]):
        out_ref[i] = total.astype(BF16)


def solve_kernel(level, slots, low, extra, outs, place_ref, source_ref, count_ref, held_ref, ahead_ref, inverse_ref,
                 *rest):
    pieces, more, outs_refs = rest[:NZ], rest[NZ : NZ + extra], rest[NZ + extra : NZ + extra + len(outs)]
    operands, total = rest[NZ + extra + len(outs) :]
    named = dict(zip(outs, outs_refs))
    nearest = pieces[0]
    chained = len(nearest.shape) == 3
    row = place_ref[0]
    operands[row] = nearest[0] if chained else nearest[...]
    for k in range(1, NZ):
        operands[lax.rem(row + NZ - k, NZ)] = pieces[k][...]
    lists = (source_ref, count_ref, held_ref)
    total[...] = nearest[1].astype(F32) if chained else jnp.zeros_like(total)
    for ref in more:
        total[...] += ref[...].astype(F32)
    add_products(total, level, slots, low, low + NZ, lambda q: operands[q], *lists)
    correction = (ahead_ref[level - 1] - total[...]).astype(BF16)
    value = dot(inverse_ref[level], correction).astype(BF16)
    named["value"][...] = value
    if "packed" in named:
        named["packed"][0] = value
        total[...] = jnp.zeros_like(total)
        add_products(total, level + 1, slots, low, low + NZ, lambda q: operands[q], *lists)
        named["packed"][1] = total[...].astype(BF16)
    if "both" in named:
        named["both"][0] = operands[row]
        named["both"][1] = value
    if "kept" in named:
        for v in range(NZ):
            named["kept"][v] = operands[v]


def later_kernel(levels, slots, low, source_ref, count_ref, held_ref, operands, *rest):
    out_refs, total = rest[:-1], rest[-1]
    for level, out_ref in zip(levels, out_refs):
        total[...] = jnp.zeros_like(total)
        add_products(total, level, slots, low, low + NZ, lambda q: operands[q], source_ref, count_ref, held_ref)
        out_ref[...] = total[...].astype(BF16)


def pair_kernel(keep_ref, got_ref, out_ref):
    out_ref[...] = (keep_ref[...] + got_ref[...].astype(F32)).astype(BF16)


def pick_kernel(column_of, place_ref, value_ref, *rest):
    got, out_ref = rest[:-1], rest[-1]
    came = got[0][...]
    for ref in got[1:]:
        came = came + ref[...]
    out_ref[...] = jnp.where(place_ref[2] == column_of, value_ref[...], came)


def pick(column_of, places, value, got, name):
    return call(
        functools.partial(pick_kernel, column_of), name, jax.ShapeDtypeStruct(value.shape, value.dtype),
        [SMEM] + [VMEM] * (1 + len(got)), (places, value, *got),
    )


def send(value, pairs):
    return lax.ppermute(value, AXES, pairs)


def to_column(value, sender, receiver, k=0):
    return send(value, [(sender * NZ + z, receiver * NZ + (z + k) % NZ) for z in range(NZ)])


def to_next_rows(value):
    return [lax.ppermute(value, "row", [(z, (z + k) % NZ) for z in range(NZ)]) for k in (1, 2, 3)]


def other_core(value):
    return lax.ppermute(value, "col", [(c, c ^ 1) for c in range(NX * NY * 2)])


def over_plane(value):
    groups = [[column(x, y, core) for y in range(NY) for x in range(NX)] for core in BOTH]
    return lax.all_to_all(value, "col", 0, 0, axis_index_groups=groups, tiled=True)


def spread_x(value, x0, core, places):
    got = [
        send(value, [(place(x0, 0, core, z), place((x0 + dx) % NX, 0, core, z)) for z in range(NZ)])
        for dx in (1, 3, 2)
    ]
    return pick(column(x0, 0, core), places, value, got, "picked")


def spread_y(value, core, here):
    got = [
        send(value, [(place(x, 0, core, z), place(x, y, core, z)) for x in range(NX) for z in range(NZ)])
        for y in (1, 3, 2)
    ]
    own = (here < 2 * NX) & (here % 2 == core)
    return lambda: jnp.where(own, value, got[0] + got[1] + got[2])


def on_device(base_rhs, base_inverse, apex, top_inverse, factor_blocks, block_source, block_count):
    levels, slots = block_source.shape[0], factor_blocks.shape[1]
    per_row, size, samples = base_rhs.shape
    shares = NX * NY
    some = size // 2 // shares
    block = factor_blocks.shape[2:]
    here, row = lax.axis_index("col"), lax.axis_index("row")
    core = here % 2
    places = jnp.stack([row, core, here]).astype(jnp.int32)
    after = lax.optimization_barrier
    one = 2 * size * size * samples
    full = jax.ShapeDtypeStruct((size, samples), BF16)

    base_solution, rounded = call(
        base_solve_kernel, "base_solve",
        (jax.ShapeDtypeStruct(base_rhs.shape, F32), jax.ShapeDtypeStruct(base_rhs.shape, BF16)),
        [VMEM, VMEM], (base_inverse, base_rhs), flops=per_row * one, nbytes=6 * base_rhs.size + 2 * base_inverse.size,
    )
    rounded, counts, places = after((rounded, block_count, places))
    pieces = [rounded] + to_next_rows(rounded)
    held, inverses = (pltpu.with_memory_space_constraint(x, pltpu.VMEM) for x in call(
        functools.partial(load_kernel, levels, slots), "load_blocks",
        (pltpu.VMEM((levels * slots,) + block, BF16), pltpu.VMEM((levels,) + block, BF16)),
        [SMEM, ANY, ANY], (counts, factor_blocks, top_inverse[:, 0]),
        scratch=[pltpu.SemaphoreType.DMA((levels * slots,)), pltpu.SemaphoreType.DMA],
        nbytes=2 * factor_blocks.size, out_specs=(VMEM, VMEM),
    ))
    lists = (block_source, block_count, held)
    keep, give = call(
        functools.partial(base_kernel, levels, slots), "base_products",
        (
            jax.ShapeDtypeStruct((shares, levels * some, samples), F32),
            jax.ShapeDtypeStruct((shares, levels * some, samples), BF16),
        ),
        [SMEM] * 3 + [VMEM] * (1 + NZ), (places, *lists, *pieces),
        scratch=[pltpu.VMEM((NZ, per_row, size, samples), BF16), pltpu.VMEM((size, samples), F32)],
        flops=levels * slots * one // 2,
    )
    pair = call(
        pair_kernel, "pair_sums", jax.ShapeDtypeStruct(give.shape, BF16), [VMEM] * 2, (keep, other_core(give))
    )
    share = call(sum_kernel, "sum_shares", jax.ShapeDtypeStruct(pair.shape, BF16), [VMEM], (over_plane(pair),))
    half = over_plane(share)
    other = other_core(half)
    ahead, first = call(
        first_kernel, "solve_0", (jax.ShapeDtypeStruct((levels - 1, size, samples), F32), full),
        [SMEM] + [VMEM] * 4, (places, half, other, apex[:, 0], inverses),
        scratch=[pltpu.VMEM((size, samples), F32)], flops=one,
    )
    two = jax.ShapeDtypeStruct((2, size, samples), BF16)
    four = jax.ShapeDtypeStruct((NZ, size, samples), BF16)
    acc = pltpu.VMEM((size, samples), F32)

    def low(u):
        return per_row * NZ + u * NZ

    def solve(u, pieces, extra, outs):
        shapes = {"value": full, "packed": two, "both": two, "kept": four}
        return call(
            functools.partial(solve_kernel, u + 1, slots, low(u), len(extra), outs), f"solve_{u + 1}",
            tuple(shapes[o] for o in outs), [SMEM] * 3 + [VMEM] * (3 + NZ + len(extra)),
            (places, *lists, ahead, inverses, *pieces, *extra),
            scratch=[pltpu.VMEM(four.shape, BF16), acc], flops=5 * one,
        )

    def products(u, levels_made, kept):
        return call(
            functools.partial(later_kernel, levels_made, slots, low(u)), f"later_{u}",
            (full,) * len(levels_made), [SMEM] * 2 + [VMEM] * 2, (*lists, kept),
            scratch=[acc], flops=4 * len(levels_made) * one,
        )

    def onward(u, value, packed):
        return [to_column(packed, u - 1, u)] + [to_column(value, u - 1, u, k) for k in (1, 2, 3)]

    x1, packed, kept = solve(0, [first] + to_next_rows(first), [], ("value", "packed", "kept"))
    pieces = onward(1, x1, packed)
    pieces, kept = after((pieces, kept))
    p30, p40 = products(0, (3, 4), kept)
    x2, packed, both, kept = solve(1, pieces, [], ("value", "packed", "both", "kept"))
    pieces = onward(2, x2, packed)
    spread12 = spread_x(both, 0, 1, places)
    p30, p40 = to_column(p30, 0, 2), to_column(p40, 0, 3)
    pieces, kept = after((pieces, kept))
    p41, = products(1, (4,), kept)
    x3, packed = solve(2, pieces, [p30], ("value", "packed"))
    pieces = onward(3, x3, packed)
    spread12 = spread_y(after((spread12, x3))[0], 1, here)
    spread3 = spread_x(x3, 1, 0, places)
    p41 = to_column(p41, 1, 3)
    x4, = solve(3, pieces, [p40, p41], ("value",))
    spread4 = spread_x(x4, 1, 1, places)
    spread3 = spread_y(after((spread3, x4))[0], 0, here)
    spread4 = spread_y(spread4, 1, here)
    out = jnp.concatenate([spread12(), spread3()[None], spread4()[None]])
    out = out + other_core(out)
    out = jnp.concatenate([first[None], out])
    return base_solution, out.astype(F32)[:, None]


def solution(mesh):
    placed = (
        P(AXES, None, None),
        P(AXES, None, None),
        P(None, "row", None, None),
        P(None, "row", None, None),
        P(None, AXES, None, None),
        P(None, AXES),
        P(None, AXES),
    )
    return jax.shard_map(
        on_device,
        mesh=mesh,
        in_specs=placed,
        out_specs=(P(AXES, None, None), P(None, "row", None, None)),
        check_vma=False,
    )
```

```python
import functools

import jax
import jax.numpy as jnp
from jax import lax
from jax.experimental import pallas as pl
from jax.experimental.pallas import tpu as pltpu
from jax.sharding import PartitionSpec as P

BF16, F32 = jnp.bfloat16, jnp.float32
AXES = ("col", "row")
NX = NY = NZ = 4
BOTH = (0, 1)
SMEM = pl.BlockSpec(memory_space=pltpu.SMEM)
VMEM = pl.BlockSpec(memory_space=pltpu.VMEM)
HBM = pl.BlockSpec(memory_space=pltpu.HBM)


def column(x, y, core):
    return (y * NX + x) * 2 + core


def place(x, y, core, z):
    return column(x, y, core) * NZ + z


def dot(a, b):
    return jnp.dot(a, b, preferred_element_type=F32)


def call(body, name, outs, in_specs, args, scratch=(), flops=0, nbytes=0, out_specs=None):
    return pl.pallas_call(
        body,
        out_shape=outs,
        in_specs=in_specs,
        out_specs=out_specs or jax.tree.map(lambda _: VMEM, outs),
        scratch_shapes=list(scratch),
        compiler_params=pltpu.CompilerParams(vmem_limit_bytes=24 * 1024 * 1024),
        cost_estimate=pl.CostEstimate(flops=flops, bytes_accessed=nbytes, transcendentals=0),
        name=name,
    )(*args)


def base_solve_kernel(inverse_ref, rhs_ref, out_ref, rounded_ref, inverse, rhs, value, sems):
    count = rhs_ref.shape[0]
    reads, writes = [], []
    for i in range(count):
        reads.append((
            pltpu.make_async_copy(inverse_ref.at[i], inverse.at[i], sems.at[0, i]),
            pltpu.make_async_copy(rhs_ref.at[i], rhs.at[i], sems.at[1, i]),
        ))
        for copy in reads[-1]:
            copy.start()
    for i in range(count):
        for copy in reads[i]:
            copy.wait()
        value[i] = dot(inverse[i], rhs[i].astype(BF16))
        writes.append(pltpu.make_async_copy(value.at[i], out_ref.at[i], sems.at[2, i]))
        writes[-1].start()
        rounded = value[i].astype(BF16)
        for v in range(rounded_ref.shape[0]):
            rounded_ref[v, i] = rounded
    for copy in writes:
        copy.wait()


def add_products(total, level, slots, low, high, operand_of, table, held_ref, ready=None):
    for slot in range(slots):
        source = table[level, slot]

        @pl.when(slot < table[level, slots])
        def _():
            if ready is not None:
                ready(level, slot).wait()

            @pl.when((source >= low) & (source < high))
            def _():
                total[...] += dot(held_ref[level * slots + slot], operand_of(source - low))


def base_kernel(levels, slots, table, factor_ref, inverse_ref, operands, keep_ref, send_ref, held_ref, kept_ref,
                total, sems, other_sem):
    def block_copy(level, slot):
        at = level * slots + slot
        return pltpu.make_async_copy(factor_ref.at[level, slot], held_ref.at[at], sems.at[at])

    for level in range(levels):
        for slot in range(slots):
            @pl.when(slot < table[level, slots])
            def _():
                block_copy(level, slot).start()
    inverses = pltpu.make_async_copy(inverse_ref, kept_ref, other_sem)
    inverses.start()
    core, per_row = table[levels, 1], operands.shape[1]
    shares, some = keep_ref.shape[0], keep_ref.shape[1] // levels
    mine = pl.multiple_of(core * shares * some, shares * some)
    other = pl.multiple_of((1 - core) * shares * some, shares * some)
    for level in range(levels):
        total[...] = jnp.zeros_like(total)
        add_products(total, level, slots, 0, NZ * per_row, lambda q: operands[q // per_row, lax.rem(q, per_row)],
                     table, held_ref, block_copy)
        for share in range(shares):
            place_in = pl.ds(level * some, some)
            keep_ref[share, place_in] = total[pl.ds(mine + share * some, some)]
            send_ref[share, place_in] = total[pl.ds(other + share * some, some)].astype(BF16)
    inverses.wait()


def first_kernel(table, half_ref, other_ref, apex_ref, inverse_ref, ahead_ref, out_ref, target):
    levels = apex_ref.shape[0]
    core = table[levels, 1]
    shares, some = half_ref.shape[0], half_ref.shape[1] // levels
    for level in range(levels):
        to = target if level == 0 else ahead_ref.at[level - 1]
        for ref, side in ((half_ref, core), (other_ref, 1 - core)):
            for share in range(shares):
                rows = pl.ds(pl.multiple_of(side * shares * some, shares * some) + share * some, some)
                to[rows] = apex_ref[level, rows] - ref[share, pl.ds(level * some, some)].astype(F32)
        if level == 0:
            out_ref[...] = dot(inverse_ref[0], target[...].astype(BF16)).astype(BF16)


def sum_kernel(in_ref, out_ref):
    total = in_ref[0].astype(F32)
    for i in range(1, in_ref.shape[0]):
        total = total + in_ref[i].astype(F32)
    for i in range(in_ref.shape[0]):
        out_ref[i] = total.astype(BF16)


def solve_kernel(level, slots, low, extra, outs, table, held_ref, ahead_ref, inverse_ref,
                 *rest):
    pieces, more, outs_refs = rest[:NZ], rest[NZ : NZ + extra], rest[NZ + extra : NZ + extra + len(outs)]
    operands, total = rest[NZ + extra + len(outs) :]
    named = dict(zip(outs, outs_refs))
    nearest = pieces[0]
    chained = len(nearest.shape) == 3
    row = table[inverse_ref.shape[0], 0]
    operands[row] = nearest[0] if chained else nearest[...]
    for k in range(1, NZ):
        operands[lax.rem(row + NZ - k, NZ)] = pieces[k][...]
    lists = (table, held_ref)
    total[...] = nearest[1].astype(F32) if chained else jnp.zeros_like(total)
    for ref in more:
        total[...] += ref[...].astype(F32)
    add_products(total, level, slots, low, low + NZ, lambda q: operands[q], *lists)
    correction = (ahead_ref[level - 1] - total[...]).astype(BF16)
    value = dot(inverse_ref[level], correction).astype(BF16)
    named["value"][...] = value
    if "packed" in named:
        named["packed"][0] = value
        total[...] = jnp.zeros_like(total)
        add_products(total, level + 1, slots, low, low + NZ, lambda q: operands[q], *lists)
        named["packed"][1] = total[...].astype(BF16)
    if "both" in named:
        named["both"][0] = operands[row]
        named["both"][1] = value
    if "kept" in named:
        for v in range(NZ):
            named["kept"][v] = operands[v]


def later_kernel(levels, slots, low, table, held_ref, operands, *rest):
    out_refs, total = rest[:-1], rest[-1]
    for level, out_ref in zip(levels, out_refs):
        total[...] = jnp.zeros_like(total)
        add_products(total, level, slots, low, low + NZ, lambda q: operands[q], table, held_ref)
        out_ref[...] = total[...].astype(BF16)


def pair_kernel(keep_ref, got_ref, out_ref):
    out_ref[...] = (keep_ref[...] + got_ref[...].astype(F32)).astype(BF16)


def pick_kernel(levels, column_of, table, value_ref, *rest):
    got, out_ref = rest[:-1], rest[-1]
    came = got[0][...]
    for ref in got[1:]:
        came = came + ref[...]
    out_ref[...] = jnp.where(table[levels, 2] == column_of, value_ref[...], came)


def pick(column_of, table, value, got, name):
    return call(
        functools.partial(pick_kernel, table.shape[0] - 1, column_of), name, jax.ShapeDtypeStruct(value.shape, value.dtype),
        [SMEM] + [VMEM] * (1 + len(got)), (table, value, *got),
    )


def send(value, pairs):
    return lax.ppermute(value, AXES, pairs)


def to_column(value, sender, receiver, k=0):
    return send(value, [(sender * NZ + z, receiver * NZ + (z + k) % NZ) for z in range(NZ)])


def other_core(value):
    return lax.ppermute(value, "col", [(c, c ^ 1) for c in range(NX * NY * 2)])


def over_plane(value):
    groups = [[column(x, y, core) for y in range(NY) for x in range(NX)] for core in BOTH]
    return lax.all_to_all(value, "col", 0, 0, axis_index_groups=groups, tiled=True)


def spread_x(value, x0, core, table):
    got = [
        send(value, [(place(x0, 0, core, z), place((x0 + dx) % NX, 0, core, z)) for z in range(NZ)])
        for dx in (1, 3, 2)
    ]
    return pick(column(x0, 0, core), table, value, got, "picked")


def spread_y(value, core, here):
    got = [
        send(value, [(place(x, 0, core, z), place(x, y, core, z)) for x in range(NX) for z in range(NZ)])
        for y in (1, 3, 2)
    ]
    own = (here < 2 * NX) & (here % 2 == core)
    return lambda: jnp.where(own, value, got[0] + got[1] + got[2])


def on_device(base_rhs, base_inverse, apex, top_inverse, factor_blocks, block_source, block_count):
    levels, slots = block_source.shape[0], factor_blocks.shape[1]
    per_row, size, samples = base_rhs.shape
    shares = NX * NY
    some = size // 2 // shares
    block = factor_blocks.shape[2:]
    here, row = lax.axis_index("col"), lax.axis_index("row")
    core = here % 2
    table = jnp.concatenate([block_source, block_count], axis=1)
    table = jnp.concatenate([table, jnp.pad(jnp.stack([row, core, here]), (0, slots - 2))[None].astype(jnp.int32)])
    after = lax.optimization_barrier
    in_hbm = functools.partial(pltpu.with_memory_space_constraint, memory_space=pltpu.HBM)
    one = 2 * size * size * samples
    full = jax.ShapeDtypeStruct((size, samples), BF16)

    base_solution, rounded = call(
        base_solve_kernel, "base_solve",
        (jax.ShapeDtypeStruct(base_rhs.shape, F32), jax.ShapeDtypeStruct((NZ,) + base_rhs.shape, BF16)),
        [HBM, HBM], (in_hbm(base_inverse), in_hbm(base_rhs)), flops=per_row * one, nbytes=6 * base_rhs.size + 2 * base_inverse.size,
        scratch=[
            pltpu.VMEM(base_inverse.shape, BF16), pltpu.VMEM(base_rhs.shape, F32), pltpu.VMEM(base_rhs.shape, F32),
            pltpu.SemaphoreType.DMA((3, per_row)),
        ],
        out_specs=(HBM, VMEM),
    )
    rounded, table = after((rounded, table))
    operands = lax.all_to_all(rounded, "row", 0, 0, tiled=True)
    keep, give, held, inverses = call(
        functools.partial(base_kernel, levels, slots), "base_products",
        (
            jax.ShapeDtypeStruct((shares, levels * some, samples), F32),
            jax.ShapeDtypeStruct((shares, levels * some, samples), BF16),
            pltpu.VMEM((levels * slots,) + block, BF16),
            pltpu.VMEM((levels,) + block, BF16),
        ),
        [SMEM, HBM, HBM, VMEM], (table, factor_blocks, in_hbm(top_inverse[:, 0]), operands),
        scratch=[
            pltpu.VMEM((size, samples), F32), pltpu.SemaphoreType.DMA((levels * slots,)), pltpu.SemaphoreType.DMA,
        ],
        flops=levels * slots * one // 2, nbytes=2 * factor_blocks.size,
    )
    held, inverses = (pltpu.with_memory_space_constraint(x, pltpu.VMEM) for x in (held, inverses))
    lists = (table, held)
    pair = call(
        pair_kernel, "pair_sums", jax.ShapeDtypeStruct(give.shape, BF16), [VMEM] * 2, (keep, other_core(give))
    )
    share = call(sum_kernel, "sum_shares", jax.ShapeDtypeStruct(pair.shape, BF16), [VMEM], (over_plane(pair),))
    half = over_plane(share)
    other = other_core(half)
    ahead, first = call(
        first_kernel, "solve_0", (jax.ShapeDtypeStruct((levels - 1, size, samples), F32), full),
        [SMEM] + [VMEM] * 4, (table, half, other, apex[:, 0], inverses),
        scratch=[pltpu.VMEM((size, samples), F32)], flops=one,
    )
    two = jax.ShapeDtypeStruct((2, size, samples), BF16)
    four = jax.ShapeDtypeStruct((NZ, size, samples), BF16)
    acc = pltpu.VMEM((size, samples), F32)

    def low(u):
        return per_row * NZ + u * NZ

    def solve(u, pieces, extra, outs):
        shapes = {"value": full, "packed": two, "both": two, "kept": four}
        return call(
            functools.partial(solve_kernel, u + 1, slots, low(u), len(extra), outs), f"solve_{u + 1}",
            tuple(shapes[o] for o in outs), [SMEM] + [VMEM] * (3 + NZ + len(extra)),
            (*lists, ahead, inverses, *pieces, *extra),
            scratch=[pltpu.VMEM(four.shape, BF16), acc], flops=5 * one,
        )

    def products(u, levels_made, kept):
        return call(
            functools.partial(later_kernel, levels_made, slots, low(u)), f"later_{u}",
            (full,) * len(levels_made), [SMEM] + [VMEM] * 2, (*lists, kept),
            scratch=[acc], flops=4 * len(levels_made) * one,
        )

    def onward(u, value, packed):
        return [to_column(packed, u - 1, u)] + [to_column(value, u - 1, u, k) for k in (1, 2, 3)]

    x1, packed, kept = solve(0, [first] + [to_column(first, 1, 0, k) for k in (1, 2, 3)], [], ("value", "packed", "kept"))
    pieces = onward(1, x1, packed)
    pieces, kept = after((pieces, kept))
    p30, p40 = products(0, (3, 4), kept)
    x2, packed, both, kept = solve(1, pieces, [], ("value", "packed", "both", "kept"))
    pieces = onward(2, x2, packed)
    spread12 = spread_x(both, 0, 1, table)
    p30, p40 = to_column(p30, 0, 2), to_column(p40, 0, 3)
    pieces, kept = after((pieces, kept))
    p41, = products(1, (4,), kept)
    x3, packed = solve(2, pieces, [p30], ("value", "packed"))
    pieces = onward(3, x3, packed)
    p41 = to_column(p41, 1, 3)
    x4, = solve(3, pieces, [p40, p41], ("value",))
    spread4 = spread_x(x4, 1, 1, table)
    spread12 = spread_y(after((spread12, x4))[0], 1, here)
    spread3 = spread_x(after((x3, x4))[0], 1, 0, table)
    spread3 = spread_y(spread3, 0, here)
    spread4 = spread_y(spread4, 1, here)
    out = jnp.concatenate([spread12(), spread3()[None], spread4()[None]])
    out = out + other_core(out)
    out = jnp.concatenate([first[None], out])
    return base_solution, out.astype(F32)[:, None]


def solution(mesh):
    placed = (
        P(AXES, None, None),
        P(AXES, None, None),
        P(None, "row", None, None),
        P(None, "row", None, None),
        P(None, AXES, None, None),
        P(None, AXES),
        P(None, AXES),
    )
    return jax.shard_map(
        on_device,
        mesh=mesh,
        in_specs=placed,
        out_specs=(P(AXES, None, None), P(None, "row", None, None)),
        check_vma=False,
    )
```

```python
import functools

import jax
import jax.numpy as jnp
from jax import lax
from jax.experimental import pallas as pl
from jax.experimental.pallas import tpu as pltpu
from jax.sharding import PartitionSpec as P

BF16, F32 = jnp.bfloat16, jnp.float32
AXES = ("col", "row")
NX = NY = NZ = 4
BOTH = (0, 1)
SMEM = pl.BlockSpec(memory_space=pltpu.SMEM)
VMEM = pl.BlockSpec(memory_space=pltpu.VMEM)
HBM = pl.BlockSpec(memory_space=pltpu.HBM)


def column(x, y, core):
    return (y * NX + x) * 2 + core


def place(x, y, core, z):
    return column(x, y, core) * NZ + z


def dot(a, b):
    return jnp.dot(a, b, preferred_element_type=F32)


def call(body, name, outs, in_specs, args, scratch=(), flops=0, nbytes=0, out_specs=None):
    return pl.pallas_call(
        body,
        out_shape=outs,
        in_specs=in_specs,
        out_specs=out_specs or jax.tree.map(lambda _: VMEM, outs),
        scratch_shapes=list(scratch),
        compiler_params=pltpu.CompilerParams(vmem_limit_bytes=24 * 1024 * 1024),
        cost_estimate=pl.CostEstimate(flops=flops, bytes_accessed=nbytes, transcendentals=0),
        name=name,
    )(*args)


def base_solve_kernel(inverse_ref, rhs_ref, out_ref, *rest):
    count = rhs_ref.shape[0]
    rounded_refs, (inverse, rhs, value, sems) = rest[:count], rest[count:]
    reads, writes = [], []
    for i in range(count):
        reads.append((
            pltpu.make_async_copy(inverse_ref.at[i], inverse.at[i], sems.at[0, i]),
            pltpu.make_async_copy(rhs_ref.at[i], rhs.at[i], sems.at[1, i]),
        ))
        for copy in reads[-1]:
            copy.start()
    for i in range(count):
        for copy in reads[i]:
            copy.wait()
        value[i] = dot(inverse[i], rhs[i].astype(BF16))
        writes.append(pltpu.make_async_copy(value.at[i], out_ref.at[i], sems.at[2, i]))
        writes[-1].start()
        rounded_refs[i][...] = value[i].astype(BF16)
    for copy in writes:
        copy.wait()


def load_kernel(levels, slots, table, factor_ref, inverse_ref, held_ref, kept_ref, sems, other_sem):
    inverses = pltpu.make_async_copy(inverse_ref, kept_ref, other_sem)
    inverses.start()

    def each(act):
        for level in range(levels):
            for slot in range(slots):
                @pl.when(slot < table[level, slots])
                def _():
                    at = level * slots + slot
                    act(pltpu.make_async_copy(factor_ref.at[level, slot], held_ref.at[at], sems.at[at]))

    each(lambda copy: copy.start())
    each(lambda copy: copy.wait())
    inverses.wait()


def add_products(total, level, slots, low, high, operand_of, table, held_ref):
    for slot in range(slots):
        source = table[level, slot]

        @pl.when((slot < table[level, slots]) & (source >= low) & (source < high))
        def _():
            total[...] += dot(held_ref[level * slots + slot], operand_of(source - low))


def base_kernel(levels, slots, table, held_ref, *rest):
    pieces, (keep_ref, send_ref, operands, total) = rest[:-4], rest[-4:]
    row, core = table[levels, 0], table[levels, 1]
    per_row = len(pieces) // NZ
    for k in range(NZ):
        for i in range(per_row):
            operands[lax.rem(row + NZ - k, NZ) * per_row + i] = pieces[k * per_row + i][...]
    shares, some = keep_ref.shape[0], keep_ref.shape[1] // levels
    mine = pl.multiple_of(core * shares * some, shares * some)
    other = pl.multiple_of((1 - core) * shares * some, shares * some)
    for level in range(levels):
        total[...] = jnp.zeros_like(total)
        add_products(total, level, slots, 0, NZ * per_row, lambda q: operands[q], table, held_ref)
        for share in range(shares):
            place_in = pl.ds(level * some, some)
            keep_ref[share, place_in] = total[pl.ds(mine + share * some, some)]
            send_ref[share, place_in] = total[pl.ds(other + share * some, some)].astype(BF16)


def first_kernel(table, half_ref, other_ref, apex_ref, inverse_ref, ahead_ref, out_ref, target):
    levels = apex_ref.shape[0]
    core = table[levels, 1]
    shares, some = half_ref.shape[0], half_ref.shape[1] // levels
    for level in range(levels):
        to = target if level == 0 else ahead_ref.at[level - 1]
        for ref, side in ((half_ref, core), (other_ref, 1 - core)):
            for share in range(shares):
                rows = pl.ds(pl.multiple_of(side * shares * some, shares * some) + share * some, some)
                to[rows] = apex_ref[level, rows] - ref[share, pl.ds(level * some, some)].astype(F32)
        if level == 0:
            out_ref[...] = dot(inverse_ref[0], target[...].astype(BF16)).astype(BF16)


def sum_kernel(in_ref, out_ref):
    total = in_ref[0].astype(F32)
    for i in range(1, in_ref.shape[0]):
        total = total + in_ref[i].astype(F32)
    for i in range(in_ref.shape[0]):
        out_ref[i] = total.astype(BF16)


def solve_kernel(level, slots, low, extra, outs, table, held_ref, ahead_ref, inverse_ref,
                 *rest):
    pieces, more, outs_refs = rest[:NZ], rest[NZ : NZ + extra], rest[NZ + extra : NZ + extra + len(outs)]
    operands, total = rest[NZ + extra + len(outs) :]
    named = dict(zip(outs, outs_refs))
    nearest = pieces[0]
    chained = len(nearest.shape) == 3
    row = table[inverse_ref.shape[0], 0]
    operands[row] = nearest[0] if chained else nearest[...]
    for k in range(1, NZ):
        operands[lax.rem(row + NZ - k, NZ)] = pieces[k][...]
    lists = (table, held_ref)
    total[...] = nearest[1].astype(F32) if chained else jnp.zeros_like(total)
    for ref in more[1 if "mixed" in named else 0 :]:
        total[...] += ref[...].astype(F32)
    add_products(total, level, slots, low, low + NZ, lambda q: operands[q], *lists)
    correction = (ahead_ref[level - 1] - total[...]).astype(BF16)
    value = dot(inverse_ref[level], correction).astype(BF16)
    named["value"][...] = value
    if "packed" in named:
        named["packed"][0] = value
        total[...] = jnp.zeros_like(total)
        add_products(total, level + 1, slots, low, low + NZ, lambda q: operands[q], *lists)
        named["packed"][1] = total[...].astype(BF16)
    if "mixed" in named:
        named["mixed"][...] = jnp.where(table[inverse_ref.shape[0], 1] == 0, more[0][...], value)
    if "kept" in named:
        for v in range(NZ):
            named["kept"][v] = operands[v]


def later_kernel(levels, slots, low, table, held_ref, operands, *rest):
    out_refs, total = rest[:-1], rest[-1]
    for level, out_ref in zip(levels, out_refs):
        total[...] = jnp.zeros_like(total)
        add_products(total, level, slots, low, low + NZ, lambda q: operands[q], table, held_ref)
        out_ref[...] = total[...].astype(BF16)


def pair_kernel(keep_ref, got_ref, out_ref):
    out_ref[...] = (keep_ref[...] + got_ref[...].astype(F32)).astype(BF16)


def pick_kernel(levels, column_of, table, value_ref, *rest):
    got, out_ref = rest[:-1], rest[-1]
    came = got[0][...]
    for ref in got[1:]:
        came = came + ref[...]
    out_ref[...] = jnp.where(table[levels, 2] // 2 == column_of // 2, value_ref[...], came)


def merge_kernel(levels, table, *rest):
    refs, out_ref = rest[:-1], rest[-1]
    each = len(refs) // out_ref.shape[0]
    for i in range(out_ref.shape[0]):
        value, *got = refs[i * each : (i + 1) * each]
        came = got[0][...]
        for ref in got[1:]:
            came = came + ref[...]
        out_ref[i] = jnp.where(table[levels, 2] < 2 * NX, value[...], came)


def final_kernel(table, first_ref, mine_ref, other_ref, out_ref):
    levels = out_ref.shape[0]
    core = table[levels, 1]
    out_ref[0] = first_ref[...].astype(F32)
    for level in range(1, levels):
        i, side = (level - 1) // 2, (level - 1) % 2
        out_ref[level] = jnp.where(core == side, mine_ref[i], other_ref[i]).astype(F32)


def pick(column_of, table, value, got):
    return call(
        functools.partial(pick_kernel, table.shape[0] - 1, column_of), "picked", jax.ShapeDtypeStruct(value.shape, value.dtype),
        [SMEM] + [VMEM] * (1 + len(got)), (table, value, *got),
    )


def send(value, pairs):
    return lax.ppermute(value, AXES, pairs)


def to_column(value, sender, receiver, k=0):
    return send(value, [(sender * NZ + z, receiver * NZ + (z + k) % NZ) for z in range(NZ)])


def to_row(value, step):
    return lax.ppermute(value, "row", [(z, (z + step) % NZ) for z in range(NZ)])


def other_core(value):
    return lax.ppermute(value, "col", [(c, c ^ 1) for c in range(NX * NY * 2)])


def over_plane(value):
    groups = [[column(x, y, core) for y in range(NY) for x in range(NX)] for core in BOTH]
    return lax.all_to_all(value, "col", 0, 0, axis_index_groups=groups, tiled=True)


def spread_x(value, x0, table):
    got = [
        send(value, [(place(x0, 0, core, z), place((x0 + dx) % NX, 0, core, z)) for core in BOTH for z in range(NZ)])
        for dx in (1, 3, 2)
    ]
    return pick(column(x0, 0, 0), table, value, got)


def spread_y(value):
    got = [
        send(value, [
            (place(x, 0, core, z), place(x, y, core, z)) for x in range(NX) for core in BOTH for z in range(NZ)
        ])
        for y in (1, 3, 2)
    ]
    return [value] + got


def on_device(base_rhs, base_inverse, apex, top_inverse, factor_blocks, block_source, block_count):
    levels, slots = block_source.shape[0], factor_blocks.shape[1]
    per_row, size, samples = base_rhs.shape
    shares = NX * NY
    some = size // 2 // shares
    block = factor_blocks.shape[2:]
    here, row = lax.axis_index("col"), lax.axis_index("row")
    core = here % 2
    table = jnp.concatenate([block_source, block_count], axis=1)
    table = jnp.concatenate([table, jnp.pad(jnp.stack([row, core, here]), (0, slots - 2))[None].astype(jnp.int32)])
    after = lax.optimization_barrier
    in_hbm = functools.partial(pltpu.with_memory_space_constraint, memory_space=pltpu.HBM)
    one = 2 * size * size * samples
    full = jax.ShapeDtypeStruct((size, samples), BF16)

    base_solution, *rounded = call(
        base_solve_kernel, "base_solve", (jax.ShapeDtypeStruct(base_rhs.shape, F32),) + (full,) * per_row,
        [HBM, HBM], (in_hbm(base_inverse), in_hbm(base_rhs)), flops=per_row * one,
        nbytes=6 * base_rhs.size + 2 * base_inverse.size,
        scratch=[
            pltpu.VMEM(base_inverse.shape, BF16), pltpu.VMEM(base_rhs.shape, F32), pltpu.VMEM(base_rhs.shape, F32),
            pltpu.SemaphoreType.DMA((3, per_row)),
        ],
        out_specs=(HBM,) + (VMEM,) * per_row,
    )
    near = [to_row(rounded[0], 1), to_row(rounded[1], -1)]
    near += [to_row(rounded[1], 1), to_row(rounded[0], -1)]
    far = [to_row(near[0], 1), to_row(near[1], -1)]
    pieces = rounded + [near[0], near[2]] + far + [near[3], near[1]]
    held, inverses = (pltpu.with_memory_space_constraint(x, pltpu.VMEM) for x in call(
        functools.partial(load_kernel, levels, slots), "load_blocks",
        (pltpu.VMEM((levels * slots,) + block, BF16), pltpu.VMEM((levels,) + block, BF16)),
        [SMEM, HBM, HBM], (table, factor_blocks, in_hbm(top_inverse[:, 0])),
        scratch=[pltpu.SemaphoreType.DMA((levels * slots,)), pltpu.SemaphoreType.DMA],
        nbytes=2 * factor_blocks.size, out_specs=(VMEM, VMEM),
    ))
    lists = (table, held)
    keep, give = call(
        functools.partial(base_kernel, levels, slots), "base_products",
        (
            jax.ShapeDtypeStruct((shares, levels * some, samples), F32),
            jax.ShapeDtypeStruct((shares, levels * some, samples), BF16),
        ),
        [SMEM] + [VMEM] * (1 + len(pieces)), (*lists, *pieces),
        scratch=[pltpu.VMEM((NZ * per_row, size, samples), BF16), pltpu.VMEM((size, samples), F32)],
        flops=levels * slots * one // 2,
    )
    pair = call(
        pair_kernel, "pair_sums", jax.ShapeDtypeStruct(give.shape, BF16), [VMEM] * 2, (keep, other_core(give))
    )
    share = call(sum_kernel, "sum_shares", jax.ShapeDtypeStruct(pair.shape, BF16), [VMEM], (over_plane(pair),))
    half = over_plane(share)
    other = other_core(half)
    ahead, first = call(
        first_kernel, "solve_0", (jax.ShapeDtypeStruct((levels - 1, size, samples), F32), full),
        [SMEM] + [VMEM] * 4, (table, half, other, apex[:, 0], inverses),
        scratch=[pltpu.VMEM((size, samples), F32)], flops=one,
    )
    two = jax.ShapeDtypeStruct((2, size, samples), BF16)
    four = jax.ShapeDtypeStruct((NZ, size, samples), BF16)
    acc = pltpu.VMEM((size, samples), F32)

    def low(u):
        return per_row * NZ + u * NZ

    def solve(u, pieces, extra, outs):
        shapes = {"value": full, "packed": two, "mixed": full, "kept": four}
        return call(
            functools.partial(solve_kernel, u + 1, slots, low(u), len(extra), outs), f"solve_{u + 1}",
            tuple(shapes[o] for o in outs), [SMEM] + [VMEM] * (3 + NZ + len(extra)),
            (*lists, ahead, inverses, *pieces, *extra),
            scratch=[pltpu.VMEM(four.shape, BF16), acc], flops=5 * one,
        )

    def products(u, levels_made, kept):
        return call(
            functools.partial(later_kernel, levels_made, slots, low(u)), f"later_{u}",
            (full,) * len(levels_made), [SMEM] + [VMEM] * 2, (*lists, kept),
            scratch=[acc], flops=4 * len(levels_made) * one,
        )

    def onward(u, value, packed):
        return [to_column(packed, u - 1, u)] + [to_column(value, u - 1, u, k) for k in (1, 2, 3)]

    x1, packed, kept = solve(0, [first] + [to_row(first, k) for k in (1, 2, 3)], [], ("value", "packed", "kept"))
    pieces = onward(1, x1, packed)
    pieces, kept = after((pieces, kept))
    p30, p40 = products(0, (3, 4), kept)
    x2, packed, mixed12, kept = solve(1, pieces, [x1], ("value", "packed", "mixed", "kept"))
    pieces = onward(2, x2, packed)
    mixed12 = spread_x(mixed12, 0, table)
    p30, p40 = to_column(p30, 0, 2), to_column(p40, 0, 3)
    pieces, kept = after((pieces, kept))
    p41, = products(1, (4,), kept)
    x3, packed = solve(2, pieces, [p30], ("value", "packed"))
    pieces = onward(3, x3, packed)
    spread12 = spread_y(after((mixed12, x3))[0])
    p41 = to_column(p41, 1, 3)
    x4, mixed34 = solve(3, pieces, [x3, p40, p41], ("value", "mixed"))
    spread34 = spread_y(spread_x(mixed34, 1, table))
    spreads = spread12 + spread34
    mine = call(
        functools.partial(merge_kernel, levels), "merged", two, [SMEM] + [VMEM] * len(spreads), (table, *spreads)
    )
    out = call(
        final_kernel, "final", jax.ShapeDtypeStruct((levels, size, samples), F32), [SMEM] + [VMEM] * 3,
        (table, first, mine, other_core(mine)),
    )
    return base_solution, out[:, None]


def solution(mesh):
    placed = (
        P(AXES, None, None),
        P(AXES, None, None),
        P(None, "row", None, None),
        P(None, "row", None, None),
        P(None, AXES, None, None),
        P(None, AXES),
        P(None, AXES),
    )
    return jax.shard_map(
        on_device,
        mesh=mesh,
        in_specs=placed,
        out_specs=(P(AXES, None, None), P(None, "row", None, None)),
        check_vma=False,
    )
```

```python
import functools

import jax
import jax.numpy as jnp
from jax import lax
from jax.experimental import pallas as pl
from jax.experimental.pallas import tpu as pltpu
from jax.sharding import PartitionSpec as P

BF16, F32 = jnp.bfloat16, jnp.float32
AXES = ("col", "row")
NX = NY = NZ = 4
BOTH = (0, 1)
SMEM = pl.BlockSpec(memory_space=pltpu.SMEM)
VMEM = pl.BlockSpec(memory_space=pltpu.VMEM)
HBM = pl.BlockSpec(memory_space=pltpu.HBM)


def column(x, y, core):
    return (y * NX + x) * 2 + core


def place(x, y, core, z):
    return column(x, y, core) * NZ + z


def dot(a, b):
    return jnp.dot(a, b, preferred_element_type=F32)


def call(body, name, outs, in_specs, args, scratch=(), flops=0, nbytes=0, out_specs=None):
    return pl.pallas_call(
        body,
        out_shape=outs,
        in_specs=in_specs,
        out_specs=out_specs or jax.tree.map(lambda _: VMEM, outs),
        scratch_shapes=list(scratch),
        compiler_params=pltpu.CompilerParams(vmem_limit_bytes=24 * 1024 * 1024),
        cost_estimate=pl.CostEstimate(flops=flops, bytes_accessed=nbytes, transcendentals=0),
        name=name,
    )(*args)


def base_solve_kernel(inverse_ref, rhs_ref, out_ref, *rest):
    count = rhs_ref.shape[0]
    rounded_refs, (inverse, rhs, value, sems) = rest[:count], rest[count:]
    reads, writes = [], []
    for i in range(count):
        reads.append((
            pltpu.make_async_copy(inverse_ref.at[i], inverse.at[i], sems.at[0, i]),
            pltpu.make_async_copy(rhs_ref.at[i], rhs.at[i], sems.at[1, i]),
        ))
        for copy in reads[-1]:
            copy.start()
    for i in range(count):
        for copy in reads[i]:
            copy.wait()
        value[i] = dot(inverse[i], rhs[i].astype(BF16))
        writes.append(pltpu.make_async_copy(value.at[i], out_ref.at[i], sems.at[2, i]))
        writes[-1].start()
        rounded_refs[i][...] = value[i].astype(BF16)
    for copy in writes:
        copy.wait()


def add_products(total, level, slots, low, high, operand_of, table, held_ref, copy_of=None):
    for slot in range(slots):
        source = table[level, slot]

        @pl.when(slot < table[level, slots])
        def _():
            if copy_of is not None:
                copy_of(level, slot).wait()

            @pl.when((source >= low) & (source < high))
            def _():
                total[...] += dot(held_ref[level * slots + slot], operand_of(source - low))


def base_kernel(levels, slots, table, factor_ref, inverse_ref, *rest):
    pieces, (keep_ref, send_ref, held_ref, kept_ref, operands, total, sems, other_sem) = rest[:-8], rest[-8:]

    def copy_of(level, slot):
        at = level * slots + slot
        return pltpu.make_async_copy(factor_ref.at[level, slot], held_ref.at[at], sems.at[at])

    for level in range(levels):
        for slot in range(slots):
            @pl.when(slot < table[level, slots])
            def _():
                copy_of(level, slot).start()
    inverses = pltpu.make_async_copy(inverse_ref, kept_ref, other_sem)
    inverses.start()
    row, core = table[levels, 0], table[levels, 1]
    per_row = len(pieces) // NZ
    for k in range(NZ):
        for i in range(per_row):
            operands[lax.rem(row + NZ - k, NZ) * per_row + i] = pieces[k * per_row + i][...]
    shares, some = keep_ref.shape[0], keep_ref.shape[1] // levels
    mine = pl.multiple_of(core * shares * some, shares * some)
    other = pl.multiple_of((1 - core) * shares * some, shares * some)
    for level in range(levels):
        total[...] = jnp.zeros_like(total)
        add_products(total, level, slots, 0, NZ * per_row, lambda q: operands[q], table, held_ref, copy_of)
        for share in range(shares):
            place_in = pl.ds(level * some, some)
            keep_ref[share, place_in] = total[pl.ds(mine + share * some, some)]
            send_ref[share, place_in] = total[pl.ds(other + share * some, some)].astype(BF16)
    inverses.wait()


def first_kernel(table, half_ref, other_ref, apex_ref, inverse_ref, ahead_ref, out_ref, target):
    levels = apex_ref.shape[0]
    core = table[levels, 1]
    shares, some = half_ref.shape[0], half_ref.shape[1] // levels
    for level in range(levels):
        to = target if level == 0 else ahead_ref.at[level - 1]
        for ref, side in ((half_ref, core), (other_ref, 1 - core)):
            for share in range(shares):
                rows = pl.ds(pl.multiple_of(side * shares * some, shares * some) + share * some, some)
                to[rows] = apex_ref[level, rows] - ref[share, pl.ds(level * some, some)].astype(F32)
        if level == 0:
            out_ref[...] = dot(inverse_ref[0], target[...].astype(BF16)).astype(BF16)


def sum_kernel(in_ref, out_ref):
    total = in_ref[0].astype(F32)
    for i in range(1, in_ref.shape[0]):
        total = total + in_ref[i].astype(F32)
    for i in range(in_ref.shape[0]):
        out_ref[i] = total.astype(BF16)


def solve_kernel(level, slots, low, extra, outs, table, held_ref, ahead_ref, inverse_ref,
                 *rest):
    pieces, more, outs_refs = rest[:NZ], rest[NZ : NZ + extra], rest[NZ + extra : NZ + extra + len(outs)]
    operands, total = rest[NZ + extra + len(outs) :]
    named = dict(zip(outs, outs_refs))
    nearest = pieces[0]
    chained = len(nearest.shape) == 3
    row = table[inverse_ref.shape[0], 0]
    operands[row] = nearest[0] if chained else nearest[...]
    for k in range(1, NZ):
        operands[lax.rem(row + NZ - k, NZ)] = pieces[k][...]
    lists = (table, held_ref)
    total[...] = nearest[1].astype(F32) if chained else jnp.zeros_like(total)
    for ref in more[1 if "mixed" in named else 0 :]:
        total[...] += ref[...].astype(F32)
    add_products(total, level, slots, low, low + NZ, lambda q: operands[q], *lists)
    correction = (ahead_ref[level - 1] - total[...]).astype(BF16)
    value = dot(inverse_ref[level], correction).astype(BF16)
    named["value"][...] = value
    if "packed" in named:
        named["packed"][0] = value
        total[...] = jnp.zeros_like(total)
        add_products(total, level + 1, slots, low, low + NZ, lambda q: operands[q], *lists)
        named["packed"][1] = total[...].astype(BF16)
    if "mixed" in named:
        named["mixed"][...] = jnp.where(table[inverse_ref.shape[0], 1] == 0, more[0][...], value)
    if "kept" in named:
        for v in range(NZ):
            named["kept"][v] = operands[v]


def later_kernel(levels, slots, low, table, held_ref, operands, *rest):
    out_refs, total = rest[:-1], rest[-1]
    for level, out_ref in zip(levels, out_refs):
        total[...] = jnp.zeros_like(total)
        add_products(total, level, slots, low, low + NZ, lambda q: operands[q], table, held_ref)
        out_ref[...] = total[...].astype(BF16)


def pair_kernel(keep_ref, got_ref, out_ref):
    out_ref[...] = (keep_ref[...] + got_ref[...].astype(F32)).astype(BF16)


def pick_kernel(levels, column_of, table, value_ref, *rest):
    got, out_ref = rest[:-1], rest[-1]
    came = got[0][...]
    for ref in got[1:]:
        came = came + ref[...]
    out_ref[...] = jnp.where(table[levels, 2] // 2 == column_of // 2, value_ref[...], came)


def merge_kernel(levels, table, *rest):
    refs, out_ref = rest[:-1], rest[-1]
    each = len(refs) // out_ref.shape[0]
    for i in range(out_ref.shape[0]):
        value, *got = refs[i * each : (i + 1) * each]
        came = got[0][...]
        for ref in got[1:]:
            came = came + ref[...]
        out_ref[i] = jnp.where(table[levels, 2] < 2 * NX, value[...], came)


def final_kernel(table, first_ref, mine_ref, other_ref, out_ref):
    levels = out_ref.shape[0]
    core = table[levels, 1]
    out_ref[0] = first_ref[...].astype(F32)
    for level in range(1, levels):
        i, side = (level - 1) // 2, (level - 1) % 2
        out_ref[level] = jnp.where(core == side, mine_ref[i], other_ref[i]).astype(F32)


def pick(column_of, table, value, got):
    return call(
        functools.partial(pick_kernel, table.shape[0] - 1, column_of), "picked", jax.ShapeDtypeStruct(value.shape, value.dtype),
        [SMEM] + [VMEM] * (1 + len(got)), (table, value, *got),
    )


def send(value, pairs):
    return lax.ppermute(value, AXES, pairs)


def to_column(value, sender, receiver, k=0):
    return send(value, [(sender * NZ + z, receiver * NZ + (z + k) % NZ) for z in range(NZ)])


def to_row(value, step):
    return lax.ppermute(value, "row", [(z, (z + step) % NZ) for z in range(NZ)])


def other_core(value):
    return lax.ppermute(value, "col", [(c, c ^ 1) for c in range(NX * NY * 2)])


def over_plane(value):
    groups = [[column(x, y, core) for y in range(NY) for x in range(NX)] for core in BOTH]
    return lax.all_to_all(value, "col", 0, 0, axis_index_groups=groups, tiled=True)


def spread_x(value, x0):
    return [value] + [
        send(value, [(place(x0, 0, core, z), place((x0 + dx) % NX, 0, core, z)) for core in BOTH for z in range(NZ)])
        for dx in (1, 3, 2)
    ]


def spread_y(value):
    got = [
        send(value, [
            (place(x, 0, core, z), place(x, y, core, z)) for x in range(NX) for core in BOTH for z in range(NZ)
        ])
        for y in (1, 3, 2)
    ]
    return [value] + got


def on_device(base_rhs, base_inverse, apex, top_inverse, factor_blocks, block_source, block_count):
    levels, slots = block_source.shape[0], factor_blocks.shape[1]
    per_row, size, samples = base_rhs.shape
    shares = NX * NY
    some = size // 2 // shares
    block = factor_blocks.shape[2:]
    here, row = lax.axis_index("col"), lax.axis_index("row")
    core = here % 2
    table = jnp.concatenate([block_source, block_count], axis=1)
    table = jnp.concatenate([table, jnp.pad(jnp.stack([row, core, here]), (0, slots - 2))[None].astype(jnp.int32)])
    after = lax.optimization_barrier
    in_hbm = functools.partial(pltpu.with_memory_space_constraint, memory_space=pltpu.HBM)
    one = 2 * size * size * samples
    full = jax.ShapeDtypeStruct((size, samples), BF16)

    base_solution, *rounded = call(
        base_solve_kernel, "base_solve", (jax.ShapeDtypeStruct(base_rhs.shape, F32),) + (full,) * per_row,
        [HBM, HBM], (in_hbm(base_inverse), in_hbm(base_rhs)), flops=per_row * one,
        nbytes=6 * base_rhs.size + 2 * base_inverse.size,
        scratch=[
            pltpu.VMEM(base_inverse.shape, BF16), pltpu.VMEM(base_rhs.shape, F32), pltpu.VMEM(base_rhs.shape, F32),
            pltpu.SemaphoreType.DMA((3, per_row)),
        ],
        out_specs=(HBM,) + (VMEM,) * per_row,
    )
    near = [to_row(rounded[0], 1), to_row(rounded[1], -1)]
    near += [to_row(rounded[1], 1), to_row(rounded[0], -1)]
    far = [to_row(near[0], 1), to_row(near[1], -1)]
    pieces = rounded + [near[0], near[2]] + far + [near[3], near[1]]
    keep, give, held, inverses = call(
        functools.partial(base_kernel, levels, slots), "base_products",
        (
            jax.ShapeDtypeStruct((shares, levels * some, samples), F32),
            jax.ShapeDtypeStruct((shares, levels * some, samples), BF16),
            pltpu.VMEM((levels * slots,) + block, BF16),
            pltpu.VMEM((levels,) + block, BF16),
        ),
        [SMEM, HBM, HBM] + [VMEM] * len(pieces), (table, factor_blocks, in_hbm(top_inverse[:, 0]), *pieces),
        scratch=[
            pltpu.VMEM((NZ * per_row, size, samples), BF16), pltpu.VMEM((size, samples), F32),
            pltpu.SemaphoreType.DMA((levels * slots,)), pltpu.SemaphoreType.DMA,
        ],
        flops=levels * slots * one // 2, nbytes=2 * factor_blocks.size,
    )
    held, inverses = (pltpu.with_memory_space_constraint(x, pltpu.VMEM) for x in (held, inverses))
    lists = (table, held)
    pair = call(
        pair_kernel, "pair_sums", jax.ShapeDtypeStruct(give.shape, BF16), [VMEM] * 2, (keep, other_core(give))
    )
    share = call(sum_kernel, "sum_shares", jax.ShapeDtypeStruct(pair.shape, BF16), [VMEM], (over_plane(pair),))
    half = over_plane(share)
    other = other_core(half)
    ahead, first = call(
        first_kernel, "solve_0", (jax.ShapeDtypeStruct((levels - 1, size, samples), F32), full),
        [SMEM] + [VMEM] * 4, (table, half, other, apex[:, 0], inverses),
        scratch=[pltpu.VMEM((size, samples), F32)], flops=one,
    )
    two = jax.ShapeDtypeStruct((2, size, samples), BF16)
    four = jax.ShapeDtypeStruct((NZ, size, samples), BF16)
    acc = pltpu.VMEM((size, samples), F32)

    def low(u):
        return per_row * NZ + u * NZ

    def solve(u, pieces, extra, outs):
        shapes = {"value": full, "packed": two, "mixed": full, "kept": four}
        return call(
            functools.partial(solve_kernel, u + 1, slots, low(u), len(extra), outs), f"solve_{u + 1}",
            tuple(shapes[o] for o in outs), [SMEM] + [VMEM] * (3 + NZ + len(extra)),
            (*lists, ahead, inverses, *pieces, *extra),
            scratch=[pltpu.VMEM(four.shape, BF16), acc], flops=5 * one,
        )

    def products(u, levels_made, kept):
        return call(
            functools.partial(later_kernel, levels_made, slots, low(u)), f"later_{u}",
            (full,) * len(levels_made), [SMEM] + [VMEM] * 2, (*lists, kept),
            scratch=[acc], flops=4 * len(levels_made) * one,
        )

    def onward(u, value, packed):
        return [to_column(packed, u - 1, u)] + [to_column(value, u - 1, u, k) for k in (1, 2, 3)]

    x1, packed, kept = solve(0, [first] + [to_row(first, k) for k in (1, 2, 3)], [], ("value", "packed", "kept"))
    pieces = onward(1, x1, packed)
    pieces, kept = after((pieces, kept))
    p30, p40 = products(0, (3, 4), kept)
    x2, packed, mixed12, kept = solve(1, pieces, [x1], ("value", "packed", "mixed", "kept"))
    pieces = onward(2, x2, packed)
    mixed12, pieces[3] = after((mixed12, pieces[3]))
    mixed12 = spread_x(mixed12, 0)
    p30, p40 = to_column(p30, 0, 2), to_column(p40, 0, 3)
    pieces, kept = after((pieces, kept))
    p41, = products(1, (4,), kept)
    pieces, mixed12 = after((pieces, mixed12))
    mixed12 = pick(column(0, 0, 0), table, mixed12[0], mixed12[1:])
    x3, packed = solve(2, pieces, [p30], ("value", "packed"))
    pieces = onward(3, x3, packed)
    mixed12, pieces[3] = after((mixed12, pieces[3]))
    spread12 = spread_y(mixed12)
    p41 = to_column(p41, 1, 3)
    pieces, spread12 = after((pieces, spread12))
    x4, mixed34 = solve(3, pieces, [x3, p40, p41], ("value", "mixed"))
    mixed34 = spread_x(mixed34, 1)
    spread34 = spread_y(pick(column(1, 0, 0), table, mixed34[0], mixed34[1:]))
    spreads = spread12 + spread34
    mine = call(
        functools.partial(merge_kernel, levels), "merged", two, [SMEM] + [VMEM] * len(spreads), (table, *spreads)
    )
    out = call(
        final_kernel, "final", jax.ShapeDtypeStruct((levels, size, samples), F32), [SMEM] + [VMEM] * 3,
        (table, first, mine, other_core(mine)),
    )
    return base_solution, out[:, None]


def solution(mesh):
    placed = (
        P(AXES, None, None),
        P(AXES, None, None),
        P(None, "row", None, None),
        P(None, "row", None, None),
        P(None, AXES, None, None),
        P(None, AXES),
        P(None, AXES),
    )
    return jax.shard_map(
        on_device,
        mesh=mesh,
        in_specs=placed,
        out_specs=(P(AXES, None, None), P(None, "row", None, None)),
        check_vma=False,
    )
```

```python
import functools

import jax
import jax.numpy as jnp
from jax import lax
from jax.experimental import pallas as pl
from jax.experimental.pallas import tpu as pltpu
from jax.sharding import PartitionSpec as P

BF16, F32 = jnp.bfloat16, jnp.float32
AXES = ("col", "row")
NX = NY = NZ = 4
BOTH = (0, 1)
SMEM = pl.BlockSpec(memory_space=pltpu.SMEM)
VMEM = pl.BlockSpec(memory_space=pltpu.VMEM)
HBM = pl.BlockSpec(memory_space=pltpu.HBM)


def column(x, y, core):
    return (y * NX + x) * 2 + core


def place(x, y, core, z):
    return column(x, y, core) * NZ + z


def dot(a, b):
    return jnp.dot(a, b, preferred_element_type=F32)


def call(body, name, outs, in_specs, args, scratch=(), flops=0, nbytes=0, out_specs=None):
    return pl.pallas_call(
        body,
        out_shape=outs,
        in_specs=in_specs,
        out_specs=out_specs or jax.tree.map(lambda _: VMEM, outs),
        scratch_shapes=list(scratch),
        compiler_params=pltpu.CompilerParams(vmem_limit_bytes=24 * 1024 * 1024),
        cost_estimate=pl.CostEstimate(flops=flops, bytes_accessed=nbytes, transcendentals=0),
        name=name,
    )(*args)


def base_solve_kernel(inverse_ref, rhs_ref, out_ref, *rest):
    count = rhs_ref.shape[0]
    rounded_refs, (inverse, rhs, value, sems) = rest[:count], rest[count:]
    reads, writes = [], []
    for i in range(count):
        reads.append((
            pltpu.make_async_copy(inverse_ref.at[i], inverse.at[i], sems.at[0, i]),
            pltpu.make_async_copy(rhs_ref.at[i], rhs.at[i], sems.at[1, i]),
        ))
        for copy in reads[-1]:
            copy.start()
    for i in range(count):
        for copy in reads[i]:
            copy.wait()
        value[i] = dot(inverse[i], rhs[i].astype(BF16))
        writes.append(pltpu.make_async_copy(value.at[i], out_ref.at[i], sems.at[2, i]))
        writes[-1].start()
        rounded_refs[i][...] = value[i].astype(BF16)
    for copy in writes:
        copy.wait()


def add_products(total, level, slots, low, high, operand_of, table, held_ref, copy_of=None):
    for slot in range(slots):
        source = table[level, slot]

        @pl.when(slot < table[level, slots])
        def _():
            if copy_of is not None:
                copy_of(level, slot).wait()

            @pl.when((source >= low) & (source < high))
            def _():
                total[...] += dot(held_ref[level * slots + slot], operand_of(source - low))


def base_kernel(levels, slots, table, factor_ref, inverse_ref, *rest):
    pieces, (keep_ref, send_ref, held_ref, kept_ref, operands, total, sems, other_sem) = rest[:-8], rest[-8:]

    def copy_of(level, slot):
        at = level * slots + slot
        return pltpu.make_async_copy(factor_ref.at[level, slot], held_ref.at[at], sems.at[at])

    for level in range(levels):
        for slot in range(slots):
            @pl.when(slot < table[level, slots])
            def _():
                copy_of(level, slot).start()
    inverses = pltpu.make_async_copy(inverse_ref, kept_ref, other_sem)
    inverses.start()
    row, core = table[levels, 0], table[levels, 1]
    per_row = len(pieces) // NZ
    for k in range(NZ):
        for i in range(per_row):
            operands[lax.rem(row + NZ - k, NZ) * per_row + i] = pieces[k * per_row + i][...]
    shares, some = keep_ref.shape[0], keep_ref.shape[1] // levels
    mine = pl.multiple_of(core * shares * some, shares * some)
    other = pl.multiple_of((1 - core) * shares * some, shares * some)
    for level in range(levels):
        total[...] = jnp.zeros_like(total)
        add_products(total, level, slots, 0, NZ * per_row, lambda q: operands[q], table, held_ref, copy_of)
        for share in range(shares):
            place_in = pl.ds(level * some, some)
            keep_ref[share, place_in] = total[pl.ds(mine + share * some, some)]
            send_ref[share, place_in] = total[pl.ds(other + share * some, some)].astype(BF16)
    inverses.wait()


def first_kernel(table, half_ref, other_ref, apex_ref, inverse_ref, ahead_ref, out_ref, target):
    levels = apex_ref.shape[0]
    core = table[levels, 1]
    shares, some = half_ref.shape[0], half_ref.shape[1] // levels
    for level in range(levels):
        to = target if level == 0 else ahead_ref.at[level - 1]
        for ref, side in ((half_ref, core), (other_ref, 1 - core)):
            for share in range(shares):
                rows = pl.ds(pl.multiple_of(side * shares * some, shares * some) + share * some, some)
                to[rows] = apex_ref[level, rows] - ref[share, pl.ds(level * some, some)].astype(F32)
        if level == 0:
            out_ref[...] = dot(inverse_ref[0], target[...].astype(BF16)).astype(BF16)


def sum_kernel(in_ref, out_ref):
    total = in_ref[0].astype(F32)
    for i in range(1, in_ref.shape[0]):
        total = total + in_ref[i].astype(F32)
    for i in range(in_ref.shape[0]):
        out_ref[i] = total.astype(BF16)


def solve_kernel(level, slots, low, extra, outs, table, held_ref, ahead_ref, inverse_ref,
                 *rest):
    pieces, more, outs_refs = rest[:NZ], rest[NZ : NZ + extra], rest[NZ + extra : NZ + extra + len(outs)]
    operands, total = rest[NZ + extra + len(outs) :]
    named = dict(zip(outs, outs_refs))
    nearest = pieces[0]
    chained = len(nearest.shape) == 3
    row = table[inverse_ref.shape[0], 0]
    operands[row] = nearest[0] if chained else nearest[...]
    for k in range(1, NZ):
        operands[lax.rem(row + NZ - k, NZ)] = pieces[k][...]
    lists = (table, held_ref)
    total[...] = nearest[1].astype(F32) if chained else jnp.zeros_like(total)
    for ref in more[1 if "mixed" in named else 0 :]:
        total[...] += ref[...].astype(F32)
    add_products(total, level, slots, low, low + NZ, lambda q: operands[q], *lists)
    correction = (ahead_ref[level - 1] - total[...]).astype(BF16)
    value = dot(inverse_ref[level], correction).astype(BF16)
    named["value"][...] = value
    if "packed" in named:
        named["packed"][0] = value
        total[...] = jnp.zeros_like(total)
        add_products(total, level + 1, slots, low, low + NZ, lambda q: operands[q], *lists)
        named["packed"][1] = total[...].astype(BF16)
    if "mixed" in named:
        named["mixed"][...] = jnp.where(table[inverse_ref.shape[0], 1] == 0, more[0][...], value)
    if "kept" in named:
        for v in range(NZ):
            named["kept"][v] = operands[v]


def later_kernel(levels, slots, low, table, held_ref, operands, *rest):
    out_refs, total = rest[:-1], rest[-1]
    for level, out_ref in zip(levels, out_refs):
        total[...] = jnp.zeros_like(total)
        add_products(total, level, slots, low, low + NZ, lambda q: operands[q], table, held_ref)
        out_ref[...] = total[...].astype(BF16)


def pair_kernel(keep_ref, got_ref, out_ref):
    out_ref[...] = (keep_ref[...] + got_ref[...].astype(F32)).astype(BF16)


def pick_kernel(levels, column_of, table, value_ref, *rest):
    got, out_ref = rest[:-1], rest[-1]
    came = got[0][...]
    for ref in got[1:]:
        came = came + ref[...]
    out_ref[...] = jnp.where(table[levels, 2] // 2 == column_of // 2, value_ref[...], came)


def merge_kernel(levels, table, *rest):
    refs, out_ref = rest[:-1], rest[-1]
    each = len(refs) // out_ref.shape[0]
    for i in range(out_ref.shape[0]):
        value, *got = refs[i * each : (i + 1) * each]
        came = got[0][...]
        for ref in got[1:]:
            came = came + ref[...]
        out_ref[i] = jnp.where(table[levels, 2] < 2 * NX, value[...], came)


def final_kernel(table, first_ref, mine_ref, other_ref, out_ref):
    levels = out_ref.shape[0]
    core = table[levels, 1]
    out_ref[0] = first_ref[...].astype(F32)
    for level in range(1, levels):
        i, side = (level - 1) // 2, (level - 1) % 2
        out_ref[level] = jnp.where(core == side, mine_ref[i], other_ref[i]).astype(F32)


def pick(column_of, table, value, got):
    return call(
        functools.partial(pick_kernel, table.shape[0] - 1, column_of), "picked", jax.ShapeDtypeStruct(value.shape, value.dtype),
        [SMEM] + [VMEM] * (1 + len(got)), (table, value, *got),
    )


def send(value, pairs):
    return lax.ppermute(value, AXES, pairs)


def to_column(value, sender, receiver, k=0):
    return send(value, [(sender * NZ + z, receiver * NZ + (z + k) % NZ) for z in range(NZ)])


def to_row(value, step):
    return lax.ppermute(value, "row", [(z, (z + step) % NZ) for z in range(NZ)])


def other_core(value):
    return lax.ppermute(value, "col", [(c, c ^ 1) for c in range(NX * NY * 2)])


def over_plane(value):
    groups = [[column(x, y, core) for y in range(NY) for x in range(NX)] for core in BOTH]
    return lax.all_to_all(value, "col", 0, 0, axis_index_groups=groups, tiled=True)


def spread_x(value, x0):
    return [value] + [
        send(value, [(place(x0, 0, core, z), place((x0 + dx) % NX, 0, core, z)) for core in BOTH for z in range(NZ)])
        for dx in (1, 3, 2)
    ]


def spread_y(value):
    got = [
        send(value, [
            (place(x, 0, core, z), place(x, y, core, z)) for x in range(NX) for core in BOTH for z in range(NZ)
        ])
        for y in (1, 3, 2)
    ]
    return [value] + got


def on_device(base_rhs, base_inverse, apex, top_inverse, factor_blocks, block_source, block_count):
    levels, slots = block_source.shape[0], factor_blocks.shape[1]
    per_row, size, samples = base_rhs.shape
    shares = NX * NY
    some = size // 2 // shares
    block = factor_blocks.shape[2:]
    here, row = lax.axis_index("col"), lax.axis_index("row")
    core = here % 2
    table = jnp.concatenate([block_source, block_count], axis=1)
    table = jnp.concatenate([table, jnp.pad(jnp.stack([row, core, here]), (0, slots - 2))[None].astype(jnp.int32)])
    after = lax.optimization_barrier
    in_hbm = functools.partial(pltpu.with_memory_space_constraint, memory_space=pltpu.HBM)
    one = 2 * size * size * samples
    full = jax.ShapeDtypeStruct((size, samples), BF16)

    base_solution, *rounded = call(
        base_solve_kernel, "base_solve", (jax.ShapeDtypeStruct(base_rhs.shape, F32),) + (full,) * per_row,
        [HBM, HBM], (in_hbm(base_inverse), in_hbm(base_rhs)), flops=per_row * one,
        nbytes=6 * base_rhs.size + 2 * base_inverse.size,
        scratch=[
            pltpu.VMEM(base_inverse.shape, BF16), pltpu.VMEM(base_rhs.shape, F32), pltpu.VMEM(base_rhs.shape, F32),
            pltpu.SemaphoreType.DMA((3, per_row)),
        ],
        out_specs=(HBM,) + (VMEM,) * per_row,
    )
    near = [to_row(rounded[0], 1), to_row(rounded[1], -1)]
    near += [to_row(rounded[1], 1), to_row(rounded[0], -1)]
    far = [to_row(near[0], 1), to_row(near[1], -1)]
    pieces = rounded + [near[0], near[2]] + far + [near[3], near[1]]
    keep, give, held, inverses = call(
        functools.partial(base_kernel, levels, slots), "base_products",
        (
            jax.ShapeDtypeStruct((shares, levels * some, samples), F32),
            jax.ShapeDtypeStruct((shares, levels * some, samples), BF16),
            pltpu.VMEM((levels * slots,) + block, BF16),
            pltpu.VMEM((levels,) + block, BF16),
        ),
        [SMEM, HBM, HBM] + [VMEM] * len(pieces), (table, factor_blocks, in_hbm(top_inverse[:, 0]), *pieces),
        scratch=[
            pltpu.VMEM((NZ * per_row, size, samples), BF16), pltpu.VMEM((size, samples), F32),
            pltpu.SemaphoreType.DMA((levels * slots,)), pltpu.SemaphoreType.DMA,
        ],
        flops=levels * slots * one // 2, nbytes=2 * factor_blocks.size,
    )
    held, inverses = (pltpu.with_memory_space_constraint(x, pltpu.VMEM) for x in (held, inverses))
    lists = (table, held)
    pair = call(
        pair_kernel, "pair_sums", jax.ShapeDtypeStruct(give.shape, BF16), [VMEM] * 2, (keep, other_core(give))
    )
    share = call(sum_kernel, "sum_shares", jax.ShapeDtypeStruct(pair.shape, BF16), [VMEM], (over_plane(pair),))
    half = over_plane(share)
    other = other_core(half)
    ahead, first = call(
        first_kernel, "solve_0", (jax.ShapeDtypeStruct((levels - 1, size, samples), F32), full),
        [SMEM] + [VMEM] * 4, (table, half, other, apex[:, 0], inverses),
        scratch=[pltpu.VMEM((size, samples), F32)], flops=one,
    )
    two = jax.ShapeDtypeStruct((2, size, samples), BF16)
    four = jax.ShapeDtypeStruct((NZ, size, samples), BF16)
    acc = pltpu.VMEM((size, samples), F32)

    def low(u):
        return per_row * NZ + u * NZ

    def solve(u, pieces, extra, outs):
        shapes = {"value": full, "packed": two, "mixed": full, "kept": four}
        return call(
            functools.partial(solve_kernel, u + 1, slots, low(u), len(extra), outs), f"solve_{u + 1}",
            tuple(shapes[o] for o in outs), [SMEM] + [VMEM] * (3 + NZ + len(extra)),
            (*lists, ahead, inverses, *pieces, *extra),
            scratch=[pltpu.VMEM(four.shape, BF16), acc], flops=5 * one,
        )

    def products(u, levels_made, kept):
        return call(
            functools.partial(later_kernel, levels_made, slots, low(u)), f"later_{u}",
            (full,) * len(levels_made), [SMEM] + [VMEM] * 2, (*lists, kept),
            scratch=[acc], flops=4 * len(levels_made) * one,
        )

    def onward(u, value, packed):
        return [to_column(packed, u - 1, u)] + [to_column(value, u - 1, u, k) for k in (1, 2, 3)]

    x1, packed, kept = solve(0, [first] + [to_row(first, k) for k in (1, 2, 3)], [], ("value", "packed", "kept"))
    pieces = onward(1, x1, packed)
    pieces, kept = after((pieces, kept))
    p30, p40 = products(0, (3, 4), kept)
    x2, packed, mixed12, kept = solve(1, pieces, [x1], ("value", "packed", "mixed", "kept"))
    pieces = onward(2, x2, packed)
    mixed12 = spread_x(mixed12, 0)
    mixed12 = pick(column(0, 0, 0), table, mixed12[0], mixed12[1:])
    p30, p40 = to_column(p30, 0, 2), to_column(p40, 0, 3)
    pieces, kept = after((pieces, kept))
    p41, = products(1, (4,), kept)
    pieces, p40 = after((pieces, p40))
    x3, packed = solve(2, pieces, [p30], ("value", "packed"))
    pieces = onward(3, x3, packed)
    spread12 = spread_y(after((mixed12, x3))[0])
    p41 = to_column(p41, 1, 3)
    x4, mixed34 = solve(3, pieces, [x3, p40, p41], ("value", "mixed"))
    mixed34 = spread_x(mixed34, 1)
    spread34 = spread_y(pick(column(1, 0, 0), table, mixed34[0], mixed34[1:]))
    spreads = spread12 + spread34
    mine = call(
        functools.partial(merge_kernel, levels), "merged", two, [SMEM] + [VMEM] * len(spreads), (table, *spreads)
    )
    out = call(
        final_kernel, "final", jax.ShapeDtypeStruct((levels, size, samples), F32), [SMEM] + [VMEM] * 3,
        (table, first, mine, other_core(mine)),
    )
    return base_solution, out[:, None]


def solution(mesh):
    placed = (
        P(AXES, None, None),
        P(AXES, None, None),
        P(None, "row", None, None),
        P(None, "row", None, None),
        P(None, AXES, None, None),
        P(None, AXES),
        P(None, AXES),
    )
    return jax.shard_map(
        on_device,
        mesh=mesh,
        in_specs=placed,
        out_specs=(P(AXES, None, None), P(None, "row", None, None)),
        check_vma=False,
    )
```

```python
import functools

import jax
import jax.numpy as jnp
from jax import lax
from jax.experimental import pallas as pl
from jax.experimental.pallas import tpu as pltpu
from jax.sharding import PartitionSpec as P

BF16, F32 = jnp.bfloat16, jnp.float32
AXES = ("col", "row")
NX = NY = NZ = 4
BOTH = (0, 1)
SMEM = pl.BlockSpec(memory_space=pltpu.SMEM)
VMEM = pl.BlockSpec(memory_space=pltpu.VMEM)
HBM = pl.BlockSpec(memory_space=pltpu.HBM)


def column(x, y, core):
    return (y * NX + x) * 2 + core


def place(x, y, core, z):
    return column(x, y, core) * NZ + z


def dot(a, b):
    return jnp.dot(a, b, preferred_element_type=F32)


def call(body, name, outs, in_specs, args, scratch=(), flops=0, nbytes=0, out_specs=None):
    return pl.pallas_call(
        body,
        out_shape=outs,
        in_specs=in_specs,
        out_specs=out_specs or jax.tree.map(lambda _: VMEM, outs),
        scratch_shapes=list(scratch),
        compiler_params=pltpu.CompilerParams(vmem_limit_bytes=24 * 1024 * 1024),
        cost_estimate=pl.CostEstimate(flops=flops, bytes_accessed=nbytes, transcendentals=0),
        name=name,
    )(*args)


def base_solve_kernel(inverse_ref, rhs_ref, out_ref, *rest):
    count = rhs_ref.shape[0]
    rounded_refs, (inverse, rhs, value, sems) = rest[:count], rest[count:]
    reads, writes = [], []
    for i in range(count):
        reads.append((
            pltpu.make_async_copy(inverse_ref.at[i], inverse.at[i], sems.at[0, i]),
            pltpu.make_async_copy(rhs_ref.at[i], rhs.at[i], sems.at[1, i]),
        ))
        for copy in reads[-1]:
            copy.start()
    for i in range(count):
        for copy in reads[i]:
            copy.wait()
        value[i] = dot(inverse[i], rhs[i].astype(BF16))
        writes.append(pltpu.make_async_copy(value.at[i], out_ref.at[i], sems.at[2, i]))
        writes[-1].start()
        rounded_refs[i][...] = value[i].astype(BF16)
    for copy in writes:
        copy.wait()


def add_products(total, level, slots, low, high, operand_of, table, held_ref, copy_of=None):
    for slot in range(slots):
        source = table[level, slot]

        @pl.when(slot < table[level, slots])
        def _():
            if copy_of is not None:
                copy_of(level, slot).wait()

            @pl.when((source >= low) & (source < high))
            def _():
                total[...] += dot(held_ref[level * slots + slot], operand_of(source - low))


def base_kernel(levels, slots, table, factor_ref, inverse_ref, *rest):
    pieces, (keep_ref, send_ref, held_ref, kept_ref, operands, total, sems, other_sem) = rest[:-8], rest[-8:]

    def copy_of(level, slot):
        at = level * slots + slot
        return pltpu.make_async_copy(factor_ref.at[level, slot], held_ref.at[at], sems.at[at])

    for level in range(levels):
        for slot in range(slots):
            @pl.when(slot < table[level, slots])
            def _():
                copy_of(level, slot).start()
    inverses = pltpu.make_async_copy(inverse_ref, kept_ref, other_sem)
    inverses.start()
    row, core = table[levels, 0], table[levels, 1]
    per_row = len(pieces) // NZ
    for k in range(NZ):
        for i in range(per_row):
            operands[lax.rem(row + NZ - k, NZ) * per_row + i] = pieces[k * per_row + i][...]
    shares, some = keep_ref.shape[0], keep_ref.shape[1] // levels
    mine = pl.multiple_of(core * shares * some, shares * some)
    other = pl.multiple_of((1 - core) * shares * some, shares * some)
    for level in range(levels):
        total[...] = jnp.zeros_like(total)
        add_products(total, level, slots, 0, NZ * per_row, lambda q: operands[q], table, held_ref, copy_of)
        for share in range(shares):
            place_in = pl.ds(level * some, some)
            keep_ref[share, place_in] = total[pl.ds(mine + share * some, some)]
            send_ref[share, place_in] = total[pl.ds(other + share * some, some)].astype(BF16)
    inverses.wait()


def first_kernel(table, half_ref, other_ref, apex_ref, inverse_ref, ahead_ref, out_ref, target):
    levels = apex_ref.shape[0]
    core = table[levels, 1]
    shares, some = half_ref.shape[0], half_ref.shape[1] // levels
    for level in range(levels):
        to = target if level == 0 else ahead_ref.at[level - 1]
        for ref, side in ((half_ref, core), (other_ref, 1 - core)):
            for share in range(shares):
                rows = pl.ds(pl.multiple_of(side * shares * some, shares * some) + share * some, some)
                to[rows] = apex_ref[level, rows] - ref[share, pl.ds(level * some, some)].astype(F32)
        if level == 0:
            out_ref[...] = dot(inverse_ref[0], target[...].astype(BF16)).astype(BF16)


def sum_kernel(in_ref, out_ref):
    total = in_ref[0].astype(F32)
    for i in range(1, in_ref.shape[0]):
        total = total + in_ref[i].astype(F32)
    for i in range(in_ref.shape[0]):
        out_ref[i] = total.astype(BF16)


def solve_kernel(level, slots, low, extra, outs, table, held_ref, ahead_ref, inverse_ref,
                 *rest):
    pieces, more, outs_refs = rest[:NZ], rest[NZ : NZ + extra], rest[NZ + extra : NZ + extra + len(outs)]
    operands, total = rest[NZ + extra + len(outs) :]
    named = dict(zip(outs, outs_refs))
    nearest = pieces[0]
    chained = len(nearest.shape) == 3
    row = table[inverse_ref.shape[0], 0]
    operands[row] = nearest[0] if chained else nearest[...]
    for k in range(1, NZ):
        operands[lax.rem(row + NZ - k, NZ)] = pieces[k][...]
    lists = (table, held_ref)
    total[...] = nearest[1].astype(F32) if chained else jnp.zeros_like(total)
    for ref in more[1 if "mixed" in named else 0 :]:
        total[...] += ref[...].astype(F32)
    add_products(total, level, slots, low, low + NZ, lambda q: operands[q], *lists)
    correction = (ahead_ref[level - 1] - total[...]).astype(BF16)
    value = dot(inverse_ref[level], correction).astype(BF16)
    named["value"][...] = value
    if "packed" in named:
        named["packed"][0] = value
        total[...] = jnp.zeros_like(total)
        add_products(total, level + 1, slots, low, low + NZ, lambda q: operands[q], *lists)
        named["packed"][1] = total[...].astype(BF16)
    if "mixed" in named:
        named["mixed"][...] = jnp.where(table[inverse_ref.shape[0], 1] == 0, more[0][...], value)
    if "kept" in named:
        for v in range(NZ):
            named["kept"][v] = operands[v]


def later_kernel(levels, slots, low, table, held_ref, operands, *rest):
    out_refs, total = rest[:-1], rest[-1]
    for level, out_ref in zip(levels, out_refs):
        total[...] = jnp.zeros_like(total)
        add_products(total, level, slots, low, low + NZ, lambda q: operands[q], table, held_ref)
        out_ref[...] = total[...].astype(BF16)


def pair_kernel(keep_ref, got_ref, out_ref):
    out_ref[...] = (keep_ref[...] + got_ref[...].astype(F32)).astype(BF16)


def pick_kernel(levels, column_of, table, value_ref, *rest):
    got, out_ref = rest[:-1], rest[-1]
    came = got[0][...]
    for ref in got[1:]:
        came = came + ref[...]
    out_ref[...] = jnp.where(table[levels, 2] // 2 == column_of // 2, value_ref[...], came)


def merge_kernel(levels, table, *rest):
    refs, out_ref = rest[:-1], rest[-1]
    each = len(refs) // out_ref.shape[0]
    for i in range(out_ref.shape[0]):
        value, *got = refs[i * each : (i + 1) * each]
        came = got[0][...]
        for ref in got[1:]:
            came = came + ref[...]
        out_ref[i] = jnp.where(table[levels, 2] < 2 * NX, value[...], came)


def final_kernel(table, first_ref, mine_ref, other_ref, out_ref):
    levels = out_ref.shape[0]
    core = table[levels, 1]
    out_ref[0] = first_ref[...].astype(F32)
    for level in range(1, levels):
        i, side = (level - 1) // 2, (level - 1) % 2
        out_ref[level] = jnp.where(core == side, mine_ref[i], other_ref[i]).astype(F32)


def pick(column_of, table, value, got):
    return call(
        functools.partial(pick_kernel, table.shape[0] - 1, column_of), "picked", jax.ShapeDtypeStruct(value.shape, value.dtype),
        [SMEM] + [VMEM] * (1 + len(got)), (table, value, *got),
    )


def send(value, pairs):
    return lax.ppermute(value, AXES, pairs)


def to_column(value, sender, receiver, k=0):
    return send(value, [(sender * NZ + z, receiver * NZ + (z + k) % NZ) for z in range(NZ)])


def to_row(value, step):
    return lax.ppermute(value, "row", [(z, (z + step) % NZ) for z in range(NZ)])


def other_core(value):
    return lax.ppermute(value, "col", [(c, c ^ 1) for c in range(NX * NY * 2)])


def over_plane(value):
    groups = [[column(x, y, core) for y in range(NY) for x in range(NX)] for core in BOTH]
    return lax.all_to_all(value, "col", 0, 0, axis_index_groups=groups, tiled=True)


def spread_x(value, x0):
    return [value] + [
        send(value, [(place(x0, 0, core, z), place((x0 + dx) % NX, 0, core, z)) for core in BOTH for z in range(NZ)])
        for dx in (1, 3, 2)
    ]


def spread_y(value):
    got = [
        send(value, [
            (place(x, 0, core, z), place(x, y, core, z)) for x in range(NX) for core in BOTH for z in range(NZ)
        ])
        for y in (1, 3, 2)
    ]
    return [value] + got


def on_device(base_rhs, base_inverse, apex, top_inverse, factor_blocks, block_source, block_count):
    levels, slots = block_source.shape[0], factor_blocks.shape[1]
    per_row, size, samples = base_rhs.shape
    shares = NX * NY
    some = size // 2 // shares
    block = factor_blocks.shape[2:]
    here, row = lax.axis_index("col"), lax.axis_index("row")
    core = here % 2
    table = jnp.concatenate([block_source, block_count], axis=1)
    table = jnp.concatenate([table, jnp.pad(jnp.stack([row, core, here]), (0, slots - 2))[None].astype(jnp.int32)])
    after = lax.optimization_barrier
    in_hbm = functools.partial(pltpu.with_memory_space_constraint, memory_space=pltpu.HBM)
    one = 2 * size * size * samples
    full = jax.ShapeDtypeStruct((size, samples), BF16)

    base_solution, *rounded = call(
        base_solve_kernel, "base_solve", (jax.ShapeDtypeStruct(base_rhs.shape, F32),) + (full,) * per_row,
        [HBM, HBM], (in_hbm(base_inverse), in_hbm(base_rhs)), flops=per_row * one,
        nbytes=6 * base_rhs.size + 2 * base_inverse.size,
        scratch=[
            pltpu.VMEM(base_inverse.shape, BF16), pltpu.VMEM(base_rhs.shape, F32), pltpu.VMEM(base_rhs.shape, F32),
            pltpu.SemaphoreType.DMA((3, per_row)),
        ],
        out_specs=(HBM,) + (VMEM,) * per_row,
    )
    near = [to_row(rounded[0], 1), to_row(rounded[1], -1)]
    near += [to_row(rounded[1], 1), to_row(rounded[0], -1)]
    far = [to_row(near[0], 1), to_row(near[1], -1)]
    pieces = rounded + [near[0], near[2]] + far + [near[3], near[1]]
    keep, give, held, inverses = call(
        functools.partial(base_kernel, levels, slots), "base_products",
        (
            jax.ShapeDtypeStruct((shares, levels * some, samples), F32),
            jax.ShapeDtypeStruct((shares, levels * some, samples), BF16),
            pltpu.VMEM((levels * slots,) + block, BF16),
            pltpu.VMEM((levels,) + block, BF16),
        ),
        [SMEM, HBM, HBM] + [VMEM] * len(pieces), (table, factor_blocks, in_hbm(top_inverse[:, 0]), *pieces),
        scratch=[
            pltpu.VMEM((NZ * per_row, size, samples), BF16), pltpu.VMEM((size, samples), F32),
            pltpu.SemaphoreType.DMA((levels * slots,)), pltpu.SemaphoreType.DMA,
        ],
        flops=levels * slots * one // 2, nbytes=2 * factor_blocks.size,
    )
    held, inverses = (pltpu.with_memory_space_constraint(x, pltpu.VMEM) for x in (held, inverses))
    lists = (table, held)
    pair = call(
        pair_kernel, "pair_sums", jax.ShapeDtypeStruct(give.shape, BF16), [VMEM] * 2, (keep, other_core(give))
    )
    share = call(sum_kernel, "sum_shares", jax.ShapeDtypeStruct(pair.shape, BF16), [VMEM], (over_plane(pair),))
    half = over_plane(share)
    other = other_core(half)
    ahead, first = call(
        first_kernel, "solve_0", (jax.ShapeDtypeStruct((levels - 1, size, samples), F32), full),
        [SMEM] + [VMEM] * 4, (table, half, other, apex[:, 0], inverses),
        scratch=[pltpu.VMEM((size, samples), F32)], flops=one,
    )
    two = jax.ShapeDtypeStruct((2, size, samples), BF16)
    four = jax.ShapeDtypeStruct((NZ, size, samples), BF16)
    acc = pltpu.VMEM((size, samples), F32)

    def low(u):
        return per_row * NZ + u * NZ

    def solve(u, pieces, extra, outs):
        shapes = {"value": full, "packed": two, "mixed": full, "kept": four}
        return call(
            functools.partial(solve_kernel, u + 1, slots, low(u), len(extra), outs), f"solve_{u + 1}",
            tuple(shapes[o] for o in outs), [SMEM] + [VMEM] * (3 + NZ + len(extra)),
            (*lists, ahead, inverses, *pieces, *extra),
            scratch=[pltpu.VMEM(four.shape, BF16), acc], flops=5 * one,
        )

    def products(u, levels_made, kept):
        return call(
            functools.partial(later_kernel, levels_made, slots, low(u)), f"later_{u}",
            (full,) * len(levels_made), [SMEM] + [VMEM] * 2, (*lists, kept),
            scratch=[acc], flops=4 * len(levels_made) * one,
        )

    def onward(u, value, packed):
        return [to_column(packed, u - 1, u)] + [to_column(value, u - 1, u, k) for k in (1, 2, 3)]

    x1, packed, kept = solve(0, [first] + [to_row(first, k) for k in (1, 2, 3)], [], ("value", "packed", "kept"))
    pieces = onward(1, x1, packed)
    pieces, kept = after((pieces, kept))
    p30, p40 = products(0, (3, 4), kept)
    x2, packed, mixed12, kept = solve(1, pieces, [x1], ("value", "packed", "mixed", "kept"))
    pieces = onward(2, x2, packed)
    mixed12 = spread_x(mixed12, 0)
    p30, p40 = to_column(p30, 0, 2), to_column(p40, 0, 3)
    pieces, kept = after((pieces, kept))
    p41, = products(1, (4,), kept)
    pieces, p40, mixed12 = after((pieces, p40, mixed12))
    mixed12 = pick(column(0, 0, 0), table, mixed12[0], mixed12[1:])
    pieces, mixed12 = after((pieces, mixed12))
    x3, packed = solve(2, pieces, [p30], ("value", "packed"))
    pieces = onward(3, x3, packed)
    p41 = to_column(p41, 1, 3)
    mixed12, x3, p41 = after((mixed12, x3, p41))
    spread12 = spread_y(mixed12)
    pieces, spread12 = after((pieces, spread12))
    x4, mixed34 = solve(3, pieces, [x3, p40, p41], ("value", "mixed"))
    mixed34 = spread_x(mixed34, 1)
    spread34 = spread_y(pick(column(1, 0, 0), table, mixed34[0], mixed34[1:]))
    spreads = spread12 + spread34
    mine = call(
        functools.partial(merge_kernel, levels), "merged", two, [SMEM] + [VMEM] * len(spreads), (table, *spreads)
    )
    out = call(
        final_kernel, "final", jax.ShapeDtypeStruct((levels, size, samples), F32), [SMEM] + [VMEM] * 3,
        (table, first, mine, other_core(mine)),
    )
    return base_solution, out[:, None]


def solution(mesh):
    placed = (
        P(AXES, None, None),
        P(AXES, None, None),
        P(None, "row", None, None),
        P(None, "row", None, None),
        P(None, AXES, None, None),
        P(None, AXES),
        P(None, AXES),
    )
    return jax.shard_map(
        on_device,
        mesh=mesh,
        in_specs=placed,
        out_specs=(P(AXES, None, None), P(None, "row", None, None)),
        check_vma=False,
    )
```

```python
import functools

import jax
import jax.numpy as jnp
from jax import lax
from jax.experimental import pallas as pl
from jax.experimental.pallas import tpu as pltpu
from jax.sharding import PartitionSpec as P

BF16, F32 = jnp.bfloat16, jnp.float32
AXES = ("col", "row")
NX = NY = NZ = 4
BOTH = (0, 1)
SMEM = pl.BlockSpec(memory_space=pltpu.SMEM)
VMEM = pl.BlockSpec(memory_space=pltpu.VMEM)
HBM = pl.BlockSpec(memory_space=pltpu.HBM)


def column(x, y, core):
    return (y * NX + x) * 2 + core


def place(x, y, core, z):
    return column(x, y, core) * NZ + z


def dot(a, b):
    return jnp.dot(a, b, preferred_element_type=F32)


def call(body, name, outs, in_specs, args, scratch=(), flops=0, nbytes=0, out_specs=None):
    return pl.pallas_call(
        body,
        out_shape=outs,
        in_specs=in_specs,
        out_specs=out_specs or jax.tree.map(lambda _: VMEM, outs),
        scratch_shapes=list(scratch),
        compiler_params=pltpu.CompilerParams(vmem_limit_bytes=24 * 1024 * 1024),
        cost_estimate=pl.CostEstimate(flops=flops, bytes_accessed=nbytes, transcendentals=0),
        name=name,
    )(*args)


def base_solve_kernel(inverse_ref, rhs_ref, out_ref, *rest):
    count = rhs_ref.shape[0]
    rounded_refs, (inverse, rhs, value, sems) = rest[:count], rest[count:]
    reads, writes = [], []
    for i in range(count):
        reads.append((
            pltpu.make_async_copy(inverse_ref.at[i], inverse.at[i], sems.at[0, i]),
            pltpu.make_async_copy(rhs_ref.at[i], rhs.at[i], sems.at[1, i]),
        ))
        for copy in reads[-1]:
            copy.start()
    for i in range(count):
        for copy in reads[i]:
            copy.wait()
        value[i] = dot(inverse[i], rhs[i].astype(BF16))
        writes.append(pltpu.make_async_copy(value.at[i], out_ref.at[i], sems.at[2, i]))
        writes[-1].start()
        rounded_refs[i][...] = value[i].astype(BF16)
    for copy in writes:
        copy.wait()


def add_products(total, level, slots, low, high, operand_of, table, held_ref, copy_of=None):
    for slot in range(slots):
        source = table[level, slot]

        @pl.when(slot < table[level, slots])
        def _():
            if copy_of is not None:
                copy_of(level, slot).wait()

            @pl.when((source >= low) & (source < high))
            def _():
                total[...] += dot(held_ref[level * slots + slot], operand_of(source - low))


def base_kernel(levels, slots, table, factor_ref, inverse_ref, *rest):
    pieces, (keep_ref, send_ref, held_ref, kept_ref, operands, total, sems, other_sem) = rest[:-8], rest[-8:]

    def copy_of(level, slot):
        at = level * slots + slot
        return pltpu.make_async_copy(factor_ref.at[level, slot], held_ref.at[at], sems.at[at])

    for level in range(levels):
        for slot in range(slots):
            @pl.when(slot < table[level, slots])
            def _():
                copy_of(level, slot).start()
    inverses = pltpu.make_async_copy(inverse_ref, kept_ref, other_sem)
    inverses.start()
    row, core = table[levels, 0], table[levels, 1]
    per_row = len(pieces) // NZ
    for k in range(NZ):
        for i in range(per_row):
            operands[lax.rem(row + NZ - k, NZ) * per_row + i] = pieces[k * per_row + i][...]
    shares, some = keep_ref.shape[0], keep_ref.shape[1] // levels
    mine = pl.multiple_of(core * shares * some, shares * some)
    other = pl.multiple_of((1 - core) * shares * some, shares * some)
    for level in range(levels):
        total[...] = jnp.zeros_like(total)
        add_products(total, level, slots, 0, NZ * per_row, lambda q: operands[q], table, held_ref, copy_of)
        for share in range(shares):
            place_in = pl.ds(level * some, some)
            keep_ref[share, place_in] = total[pl.ds(mine + share * some, some)]
            send_ref[share, place_in] = total[pl.ds(other + share * some, some)].astype(BF16)
    inverses.wait()


def first_kernel(table, half_ref, other_ref, apex_ref, inverse_ref, ahead_ref, out_ref, target):
    levels = apex_ref.shape[0]
    core = table[levels, 1]
    shares, some = half_ref.shape[0], half_ref.shape[1] // levels
    for level in range(levels):
        to = target if level == 0 else ahead_ref.at[level - 1]
        for ref, side in ((half_ref, core), (other_ref, 1 - core)):
            for share in range(shares):
                rows = pl.ds(pl.multiple_of(side * shares * some, shares * some) + share * some, some)
                to[rows] = apex_ref[level, rows] - ref[share, pl.ds(level * some, some)].astype(F32)
        if level == 0:
            out_ref[...] = dot(inverse_ref[0], target[...].astype(BF16)).astype(BF16)


def sum_kernel(in_ref, out_ref):
    total = in_ref[0].astype(F32)
    for i in range(1, in_ref.shape[0]):
        total = total + in_ref[i].astype(F32)
    for i in range(in_ref.shape[0]):
        out_ref[i] = total.astype(BF16)


def solve_kernel(level, slots, low, extra, outs, table, held_ref, ahead_ref, inverse_ref,
                 *rest):
    pieces, more, outs_refs = rest[:NZ], rest[NZ : NZ + extra], rest[NZ + extra : NZ + extra + len(outs)]
    operands, total = rest[NZ + extra + len(outs) :]
    named = dict(zip(outs, outs_refs))
    nearest = pieces[0]
    chained = len(nearest.shape) == 3
    row = table[inverse_ref.shape[0], 0]
    operands[row] = nearest[0] if chained else nearest[...]
    for k in range(1, NZ):
        operands[lax.rem(row + NZ - k, NZ)] = pieces[k][...]
    lists = (table, held_ref)
    total[...] = nearest[1].astype(F32) if chained else jnp.zeros_like(total)
    for ref in more[1 if "mixed" in named else 0 :]:
        total[...] += (ref[0] if len(ref.shape) == 3 else ref[...]).astype(F32)
    add_products(total, level, slots, low, low + NZ, lambda q: operands[q], *lists)
    correction = (ahead_ref[level - 1] - total[...]).astype(BF16)
    value = dot(inverse_ref[level], correction).astype(BF16)
    named["value"][...] = value
    if "packed" in named:
        named["packed"][0] = value
        carried = [ref for ref in more if len(ref.shape) == 3]
        total[...] = carried[0][1].astype(F32) if carried else jnp.zeros_like(total)
        add_products(total, level + 1, slots, low, low + NZ, lambda q: operands[q], *lists)
        named["packed"][1] = total[...].astype(BF16)
    if "mixed" in named:
        named["mixed"][...] = jnp.where(table[inverse_ref.shape[0], 1] == 0, more[0][...], value)
    if "kept" in named:
        for v in range(NZ):
            named["kept"][v] = operands[v]


def later_kernel(levels, slots, low, table, held_ref, operands, out_ref, total):
    for i, level in enumerate(levels):
        total[...] = jnp.zeros_like(total)
        add_products(total, level, slots, low, low + NZ, lambda q: operands[q], table, held_ref)
        out_ref[i] = total[...].astype(BF16)


def pair_kernel(keep_ref, got_ref, out_ref):
    out_ref[...] = (keep_ref[...] + got_ref[...].astype(F32)).astype(BF16)


def pick_kernel(levels, column_of, table, value_ref, *rest):
    got, out_ref = rest[:-1], rest[-1]
    came = got[0][...]
    for ref in got[1:]:
        came = came + ref[...]
    out_ref[...] = jnp.where(table[levels, 2] // 2 == column_of // 2, value_ref[...], came)


def merge_kernel(levels, table, *rest):
    refs, out_ref = rest[:-1], rest[-1]
    each = len(refs) // out_ref.shape[0]
    for i in range(out_ref.shape[0]):
        value, *got = refs[i * each : (i + 1) * each]
        came = got[0][...]
        for ref in got[1:]:
            came = came + ref[...]
        out_ref[i] = jnp.where(table[levels, 2] < 2 * NX, value[...], came)


def final_kernel(table, first_ref, mine_ref, other_ref, out_ref):
    levels = out_ref.shape[0]
    core = table[levels, 1]
    out_ref[0] = first_ref[...].astype(F32)
    for level in range(1, levels):
        i, side = (level - 1) // 2, (level - 1) % 2
        out_ref[level] = jnp.where(core == side, mine_ref[i], other_ref[i]).astype(F32)


def pick(column_of, table, value, got):
    return call(
        functools.partial(pick_kernel, table.shape[0] - 1, column_of), "picked", jax.ShapeDtypeStruct(value.shape, value.dtype),
        [SMEM] + [VMEM] * (1 + len(got)), (table, value, *got),
    )


def send(value, pairs):
    return lax.ppermute(value, AXES, pairs)


def to_column(value, sender, receiver, k=0):
    return send(value, [(sender * NZ + z, receiver * NZ + (z + k) % NZ) for z in range(NZ)])


def to_row(value, step):
    return lax.ppermute(value, "row", [(z, (z + step) % NZ) for z in range(NZ)])


def other_core(value):
    return lax.ppermute(value, "col", [(c, c ^ 1) for c in range(NX * NY * 2)])


def over_plane(value):
    groups = [[column(x, y, core) for y in range(NY) for x in range(NX)] for core in BOTH]
    return lax.all_to_all(value, "col", 0, 0, axis_index_groups=groups, tiled=True)


def spread_x(value, x0):
    return [value] + [
        send(value, [(place(x0, 0, core, z), place((x0 + dx) % NX, 0, core, z)) for core in BOTH for z in range(NZ)])
        for dx in (1, 3, 2)
    ]


def spread_y(value):
    got = [
        send(value, [
            (place(x, 0, core, z), place(x, y, core, z)) for x in range(NX) for core in BOTH for z in range(NZ)
        ])
        for y in (1, 3, 2)
    ]
    return [value] + got


def on_device(base_rhs, base_inverse, apex, top_inverse, factor_blocks, block_source, block_count):
    levels, slots = block_source.shape[0], factor_blocks.shape[1]
    per_row, size, samples = base_rhs.shape
    shares = NX * NY
    some = size // 2 // shares
    block = factor_blocks.shape[2:]
    here, row = lax.axis_index("col"), lax.axis_index("row")
    core = here % 2
    table = jnp.concatenate([block_source, block_count], axis=1)
    table = jnp.concatenate([table, jnp.pad(jnp.stack([row, core, here]), (0, slots - 2))[None].astype(jnp.int32)])
    after = lax.optimization_barrier
    in_hbm = functools.partial(pltpu.with_memory_space_constraint, memory_space=pltpu.HBM)
    one = 2 * size * size * samples
    full = jax.ShapeDtypeStruct((size, samples), BF16)

    base_solution, *rounded = call(
        base_solve_kernel, "base_solve", (jax.ShapeDtypeStruct(base_rhs.shape, F32),) + (full,) * per_row,
        [HBM, HBM], (in_hbm(base_inverse), in_hbm(base_rhs)), flops=per_row * one,
        nbytes=6 * base_rhs.size + 2 * base_inverse.size,
        scratch=[
            pltpu.VMEM(base_inverse.shape, BF16), pltpu.VMEM(base_rhs.shape, F32), pltpu.VMEM(base_rhs.shape, F32),
            pltpu.SemaphoreType.DMA((3, per_row)),
        ],
        out_specs=(HBM,) + (VMEM,) * per_row,
    )
    near = [to_row(rounded[0], 1), to_row(rounded[1], -1)]
    near += [to_row(rounded[1], 1), to_row(rounded[0], -1)]
    far = [to_row(near[0], 1), to_row(near[1], -1)]
    pieces = rounded + [near[0], near[2]] + far + [near[3], near[1]]
    keep, give, held, inverses = call(
        functools.partial(base_kernel, levels, slots), "base_products",
        (
            jax.ShapeDtypeStruct((shares, levels * some, samples), F32),
            jax.ShapeDtypeStruct((shares, levels * some, samples), BF16),
            pltpu.VMEM((levels * slots,) + block, BF16),
            pltpu.VMEM((levels,) + block, BF16),
        ),
        [SMEM, HBM, HBM] + [VMEM] * len(pieces), (table, factor_blocks, in_hbm(top_inverse[:, 0]), *pieces),
        scratch=[
            pltpu.VMEM((NZ * per_row, size, samples), BF16), pltpu.VMEM((size, samples), F32),
            pltpu.SemaphoreType.DMA((levels * slots,)), pltpu.SemaphoreType.DMA,
        ],
        flops=levels * slots * one // 2, nbytes=2 * factor_blocks.size,
    )
    held, inverses = (pltpu.with_memory_space_constraint(x, pltpu.VMEM) for x in (held, inverses))
    lists = (table, held)
    pair = call(
        pair_kernel, "pair_sums", jax.ShapeDtypeStruct(give.shape, BF16), [VMEM] * 2, (keep, other_core(give))
    )
    share = call(sum_kernel, "sum_shares", jax.ShapeDtypeStruct(pair.shape, BF16), [VMEM], (over_plane(pair),))
    half = over_plane(share)
    other = other_core(half)
    ahead, first = call(
        first_kernel, "solve_0", (jax.ShapeDtypeStruct((levels - 1, size, samples), F32), full),
        [SMEM] + [VMEM] * 4, (table, half, other, apex[:, 0], inverses),
        scratch=[pltpu.VMEM((size, samples), F32)], flops=one,
    )
    two = jax.ShapeDtypeStruct((2, size, samples), BF16)
    four = jax.ShapeDtypeStruct((NZ, size, samples), BF16)
    acc = pltpu.VMEM((size, samples), F32)

    def low(u):
        return per_row * NZ + u * NZ

    def solve(u, pieces, extra, outs):
        shapes = {"value": full, "packed": two, "mixed": full, "kept": four}
        return call(
            functools.partial(solve_kernel, u + 1, slots, low(u), len(extra), outs), f"solve_{u + 1}",
            tuple(shapes[o] for o in outs), [SMEM] + [VMEM] * (3 + NZ + len(extra)),
            (*lists, ahead, inverses, *pieces, *extra),
            scratch=[pltpu.VMEM(four.shape, BF16), acc], flops=5 * one,
        )

    def products(u, levels_made, kept):
        return call(
            functools.partial(later_kernel, levels_made, slots, low(u)), f"later_{u}",
            jax.ShapeDtypeStruct((len(levels_made), size, samples), BF16), [SMEM] + [VMEM] * 2, (*lists, kept),
            scratch=[acc], flops=4 * len(levels_made) * one,
        )

    def onward(u, value, packed):
        return [to_column(packed, u - 1, u)] + [to_column(value, u - 1, u, k) for k in (1, 2, 3)]

    x1, packed, kept = solve(0, [first] + [to_row(first, k) for k in (1, 2, 3)], [], ("value", "packed", "kept"))
    pieces = onward(1, x1, packed)
    pieces, kept = after((pieces, kept))
    carried = products(0, (3, 4), kept)
    x2, packed, mixed12, kept = solve(1, pieces, [x1], ("value", "packed", "mixed", "kept"))
    pieces = onward(2, x2, packed)
    mixed12 = spread_x(mixed12, 0)
    mixed12 = pick(column(0, 0, 0), table, mixed12[0], mixed12[1:])
    carried = to_column(carried, 0, 2)
    pieces, kept = after((pieces, kept))
    p41 = products(1, (4,), kept)
    x3, packed = solve(2, pieces, [carried], ("value", "packed"))
    pieces = onward(3, x3, packed)
    spread12 = spread_y(after((mixed12, x3))[0])
    p41 = to_column(p41, 1, 3)
    x4, mixed34 = solve(3, pieces, [x3, p41], ("value", "mixed"))
    mixed34 = spread_x(mixed34, 1)
    spread34 = spread_y(pick(column(1, 0, 0), table, mixed34[0], mixed34[1:]))
    spreads = spread12 + spread34
    mine = call(
        functools.partial(merge_kernel, levels), "merged", two, [SMEM] + [VMEM] * len(spreads), (table, *spreads)
    )
    out = call(
        final_kernel, "final", jax.ShapeDtypeStruct((levels, size, samples), F32), [SMEM] + [VMEM] * 3,
        (table, first, mine, other_core(mine)),
    )
    return base_solution, out[:, None]


def solution(mesh):
    placed = (
        P(AXES, None, None),
        P(AXES, None, None),
        P(None, "row", None, None),
        P(None, "row", None, None),
        P(None, AXES, None, None),
        P(None, AXES),
        P(None, AXES),
    )
    return jax.shard_map(
        on_device,
        mesh=mesh,
        in_specs=placed,
        out_specs=(P(AXES, None, None), P(None, "row", None, None)),
        check_vma=False,
    )
```

```python
import functools

import jax
import jax.numpy as jnp
from jax import lax
from jax.experimental import pallas as pl
from jax.experimental.pallas import tpu as pltpu
from jax.sharding import PartitionSpec as P

BF16, F32 = jnp.bfloat16, jnp.float32
AXES = ("col", "row")
NX = NY = NZ = 4
BOTH = (0, 1)
SMEM = pl.BlockSpec(memory_space=pltpu.SMEM)
VMEM = pl.BlockSpec(memory_space=pltpu.VMEM)
HBM = pl.BlockSpec(memory_space=pltpu.HBM)


def column(x, y, core):
    return (y * NX + x) * 2 + core


def place(x, y, core, z):
    return column(x, y, core) * NZ + z


def dot(a, b):
    return jnp.dot(a, b, preferred_element_type=F32)


def call(body, name, outs, in_specs, args, scratch=(), flops=0, nbytes=0, out_specs=None):
    return pl.pallas_call(
        body,
        out_shape=outs,
        in_specs=in_specs,
        out_specs=out_specs or jax.tree.map(lambda _: VMEM, outs),
        scratch_shapes=list(scratch),
        compiler_params=pltpu.CompilerParams(vmem_limit_bytes=24 * 1024 * 1024),
        cost_estimate=pl.CostEstimate(flops=flops, bytes_accessed=nbytes, transcendentals=0),
        name=name,
    )(*args)


def base_solve_kernel(inverse_ref, rhs_ref, out_ref, *rest):
    count = rhs_ref.shape[0]
    rounded_refs, (inverse, rhs, value, sems) = rest[:count], rest[count:]
    reads, writes = [], []
    for i in range(count):
        reads.append((
            pltpu.make_async_copy(inverse_ref.at[i], inverse.at[i], sems.at[0, i]),
            pltpu.make_async_copy(rhs_ref.at[i], rhs.at[i], sems.at[1, i]),
        ))
        for copy in reads[-1]:
            copy.start()
    for i in range(count):
        for copy in reads[i]:
            copy.wait()
        value[i] = dot(inverse[i], rhs[i].astype(BF16))
        writes.append(pltpu.make_async_copy(value.at[i], out_ref.at[i], sems.at[2, i]))
        writes[-1].start()
        rounded_refs[i][...] = value[i].astype(BF16)
    for copy in writes:
        copy.wait()


def add_products(total, level, slots, low, high, operand_of, table, held_ref, copy_of=None):
    for slot in range(slots):
        source = table[level, slot]

        @pl.when(slot < table[level, slots])
        def _():
            if copy_of is not None:
                copy_of(level, slot).wait()

            @pl.when((source >= low) & (source < high))
            def _():
                total[...] += dot(held_ref[level * slots + slot], operand_of(source - low))


def base_kernel(levels, slots, table, factor_ref, inverse_ref, *rest):
    pieces, (keep_ref, send_ref, held_ref, kept_ref, operands, total, sems, other_sem) = rest[:-8], rest[-8:]

    def copy_of(level, slot):
        at = level * slots + slot
        return pltpu.make_async_copy(factor_ref.at[level, slot], held_ref.at[at], sems.at[at])

    for level in range(levels):
        for slot in range(slots):
            @pl.when(slot < table[level, slots])
            def _():
                copy_of(level, slot).start()
    inverses = pltpu.make_async_copy(inverse_ref, kept_ref, other_sem)
    inverses.start()
    row, core = table[levels, 0], table[levels, 1]
    per_row = len(pieces) // NZ
    for k in range(NZ):
        for i in range(per_row):
            operands[lax.rem(row + NZ - k, NZ) * per_row + i] = pieces[k * per_row + i][...]
    shares, some = keep_ref.shape[0], keep_ref.shape[1] // levels
    mine = pl.multiple_of(core * shares * some, shares * some)
    other = pl.multiple_of((1 - core) * shares * some, shares * some)
    for level in range(levels):
        total[...] = jnp.zeros_like(total)
        add_products(total, level, slots, 0, NZ * per_row, lambda q: operands[q], table, held_ref, copy_of)
        for share in range(shares):
            place_in = pl.ds(level * some, some)
            keep_ref[share, place_in] = total[pl.ds(mine + share * some, some)]
            send_ref[share, place_in] = total[pl.ds(other + share * some, some)].astype(BF16)
    inverses.wait()


def first_kernel(table, half_ref, other_ref, apex_ref, inverse_ref, ahead_ref, out_ref, target):
    levels = apex_ref.shape[0]
    core = table[levels, 1]
    shares, some = half_ref.shape[0], half_ref.shape[1] // levels
    for level in range(levels):
        to = target if level == 0 else ahead_ref.at[level - 1]
        for ref, side in ((half_ref, core), (other_ref, 1 - core)):
            for share in range(shares):
                rows = pl.ds(pl.multiple_of(side * shares * some, shares * some) + share * some, some)
                to[rows] = apex_ref[level, rows] - ref[share, pl.ds(level * some, some)].astype(F32)
        if level == 0:
            out_ref[...] = dot(inverse_ref[0], target[...].astype(BF16)).astype(BF16)


def sum_kernel(in_ref, out_ref):
    total = in_ref[0].astype(F32)
    for i in range(1, in_ref.shape[0]):
        total = total + in_ref[i].astype(F32)
    for i in range(in_ref.shape[0]):
        out_ref[i] = total.astype(BF16)


def solve_kernel(level, slots, low, extra, outs, table, held_ref, ahead_ref, inverse_ref,
                 *rest):
    pieces, more, outs_refs = rest[:NZ], rest[NZ : NZ + extra], rest[NZ + extra : NZ + extra + len(outs)]
    operands, total = rest[NZ + extra + len(outs) :]
    named = dict(zip(outs, outs_refs))
    nearest = pieces[0]
    chained = len(nearest.shape) == 3
    row = table[inverse_ref.shape[0], 0]
    operands[row] = nearest[0] if chained else nearest[...]
    for k in range(1, NZ):
        operands[lax.rem(row + NZ - k, NZ)] = pieces[k][...]
    lists = (table, held_ref)
    total[...] = nearest[1].astype(F32) if chained else jnp.zeros_like(total)
    for ref in more[1 if "mixed" in named else 0 :]:
        total[...] += (ref[0] if len(ref.shape) == 3 else ref[...]).astype(F32)
    add_products(total, level, slots, low, low + NZ, lambda q: operands[q], *lists)
    correction = (ahead_ref[level - 1] - total[...]).astype(BF16)
    value = dot(inverse_ref[level], correction).astype(BF16)
    named["value"][...] = value
    if "packed" in named:
        named["packed"][0] = value
        carried = [ref for ref in more if len(ref.shape) == 3]
        total[...] = carried[0][1].astype(F32) if carried else jnp.zeros_like(total)
        add_products(total, level + 1, slots, low, low + NZ, lambda q: operands[q], *lists)
        named["packed"][1] = total[...].astype(BF16)
    if "mixed" in named:
        named["mixed"][...] = jnp.where(table[inverse_ref.shape[0], 1] == 0, more[0][...], value)
    if "kept" in named:
        for v in range(NZ):
            named["kept"][v] = operands[v]


def later_kernel(levels, slots, low, table, held_ref, operands, out_ref, total):
    for i, level in enumerate(levels):
        total[...] = jnp.zeros_like(total)
        add_products(total, level, slots, low, low + NZ, lambda q: operands[q], table, held_ref)
        out_ref[i] = total[...].astype(BF16)


def pair_kernel(keep_ref, got_ref, out_ref):
    out_ref[...] = (keep_ref[...] + got_ref[...].astype(F32)).astype(BF16)


def pick_kernel(levels, column_of, table, value_ref, *rest):
    got, out_ref = rest[:-1], rest[-1]
    came = got[0][...]
    for ref in got[1:]:
        came = came + ref[...]
    out_ref[...] = jnp.where(table[levels, 2] // 2 == column_of // 2, value_ref[...], came)


def merge_kernel(levels, table, *rest):
    refs, out_ref = rest[:-1], rest[-1]
    each = len(refs) // out_ref.shape[0]
    for i in range(out_ref.shape[0]):
        value, *got = refs[i * each : (i + 1) * each]
        came = got[0][...]
        for ref in got[1:]:
            came = came + ref[...]
        out_ref[i] = jnp.where(table[levels, 2] < 2 * NX, value[...], came)


def final_kernel(table, first_ref, mine_ref, other_ref, out_ref):
    levels = out_ref.shape[0]
    core = table[levels, 1]
    out_ref[0] = first_ref[...].astype(F32)
    for level in range(1, levels):
        i, side = (level - 1) // 2, (level - 1) % 2
        out_ref[level] = jnp.where(core == side, mine_ref[i], other_ref[i]).astype(F32)


def pick(column_of, table, value, got):
    return call(
        functools.partial(pick_kernel, table.shape[0] - 1, column_of), "picked", jax.ShapeDtypeStruct(value.shape, value.dtype),
        [SMEM] + [VMEM] * (1 + len(got)), (table, value, *got),
    )


def send(value, pairs):
    return lax.ppermute(value, AXES, pairs)


def to_column(value, sender, receiver, k=0):
    return send(value, [(sender * NZ + z, receiver * NZ + (z + k) % NZ) for z in range(NZ)])


def to_row(value, step):
    return lax.ppermute(value, "row", [(z, (z + step) % NZ) for z in range(NZ)])


def other_core(value):
    return lax.ppermute(value, "col", [(c, c ^ 1) for c in range(NX * NY * 2)])


def over_plane(value):
    groups = [[column(x, y, core) for y in range(NY) for x in range(NX)] for core in BOTH]
    return lax.all_to_all(value, "col", 0, 0, axis_index_groups=groups, tiled=True)


def spread_x(value, x0):
    return [value] + [
        send(value, [(place(x0, 0, core, z), place((x0 + dx) % NX, 0, core, z)) for core in BOTH for z in range(NZ)])
        for dx in (1, 3, 2)
    ]


def spread_y(value):
    got = [
        send(value, [
            (place(x, 0, core, z), place(x, y, core, z)) for x in range(NX) for core in BOTH for z in range(NZ)
        ])
        for y in (1, 3, 2)
    ]
    return [value] + got


def on_device(base_rhs, base_inverse, apex, top_inverse, factor_blocks, block_source, block_count):
    levels, slots = block_source.shape[0], factor_blocks.shape[1]
    per_row, size, samples = base_rhs.shape
    shares = NX * NY
    some = size // 2 // shares
    block = factor_blocks.shape[2:]
    here, row = lax.axis_index("col"), lax.axis_index("row")
    core = here % 2
    table = jnp.concatenate([block_source, block_count], axis=1)
    table = jnp.concatenate([table, jnp.pad(jnp.stack([row, core, here]), (0, slots - 2))[None].astype(jnp.int32)])
    after = lax.optimization_barrier
    in_hbm = functools.partial(pltpu.with_memory_space_constraint, memory_space=pltpu.HBM)
    one = 2 * size * size * samples
    full = jax.ShapeDtypeStruct((size, samples), BF16)

    base_solution, *rounded = call(
        base_solve_kernel, "base_solve", (jax.ShapeDtypeStruct(base_rhs.shape, F32),) + (full,) * per_row,
        [HBM, HBM], (in_hbm(base_inverse), in_hbm(base_rhs)), flops=per_row * one,
        nbytes=6 * base_rhs.size + 2 * base_inverse.size,
        scratch=[
            pltpu.VMEM(base_inverse.shape, BF16), pltpu.VMEM(base_rhs.shape, F32), pltpu.VMEM(base_rhs.shape, F32),
            pltpu.SemaphoreType.DMA((3, per_row)),
        ],
        out_specs=(HBM,) + (VMEM,) * per_row,
    )
    near = [to_row(rounded[0], 1), to_row(rounded[1], -1)]
    near += [to_row(rounded[1], 1), to_row(rounded[0], -1)]
    far = [to_row(near[0], 1), to_row(near[1], -1)]
    pieces = rounded + [near[0], near[2]] + far + [near[3], near[1]]
    keep, give, held, inverses = call(
        functools.partial(base_kernel, levels, slots), "base_products",
        (
            jax.ShapeDtypeStruct((shares, levels * some, samples), F32),
            jax.ShapeDtypeStruct((shares, levels * some, samples), BF16),
            pltpu.VMEM((levels * slots,) + block, BF16),
            pltpu.VMEM((levels,) + block, BF16),
        ),
        [SMEM, HBM, HBM] + [VMEM] * len(pieces), (table, factor_blocks, in_hbm(top_inverse[:, 0]), *pieces),
        scratch=[
            pltpu.VMEM((NZ * per_row, size, samples), BF16), pltpu.VMEM((size, samples), F32),
            pltpu.SemaphoreType.DMA((levels * slots,)), pltpu.SemaphoreType.DMA,
        ],
        flops=levels * slots * one // 2, nbytes=2 * factor_blocks.size,
    )
    held, inverses = (pltpu.with_memory_space_constraint(x, pltpu.VMEM) for x in (held, inverses))
    lists = (table, held)
    pair = call(
        pair_kernel, "pair_sums", jax.ShapeDtypeStruct(give.shape, BF16), [VMEM] * 2, (keep, other_core(give))
    )
    share = call(sum_kernel, "sum_shares", jax.ShapeDtypeStruct(pair.shape, BF16), [VMEM], (over_plane(pair),))
    half = over_plane(share)
    other = other_core(half)
    ahead, first = call(
        first_kernel, "solve_0", (jax.ShapeDtypeStruct((levels - 1, size, samples), F32), full),
        [SMEM] + [VMEM] * 4, (table, half, other, apex[:, 0], inverses),
        scratch=[pltpu.VMEM((size, samples), F32)], flops=one,
    )
    two = jax.ShapeDtypeStruct((2, size, samples), BF16)
    four = jax.ShapeDtypeStruct((NZ, size, samples), BF16)
    acc = pltpu.VMEM((size, samples), F32)

    def low(u):
        return per_row * NZ + u * NZ

    def solve(u, pieces, extra, outs):
        shapes = {"value": full, "packed": two, "mixed": full, "kept": four}
        return call(
            functools.partial(solve_kernel, u + 1, slots, low(u), len(extra), outs), f"solve_{u + 1}",
            tuple(shapes[o] for o in outs), [SMEM] + [VMEM] * (3 + NZ + len(extra)),
            (*lists, ahead, inverses, *pieces, *extra),
            scratch=[pltpu.VMEM(four.shape, BF16), acc], flops=5 * one,
        )

    def products(u, levels_made, kept):
        return call(
            functools.partial(later_kernel, levels_made, slots, low(u)), f"later_{u}",
            jax.ShapeDtypeStruct((len(levels_made), size, samples), BF16), [SMEM] + [VMEM] * 2, (*lists, kept),
            scratch=[acc], flops=4 * len(levels_made) * one,
        )

    def onward(u, value, packed):
        return [to_column(packed, u - 1, u)] + [to_column(value, u - 1, u, k) for k in (1, 2, 3)]

    x1, packed, kept = solve(0, [first] + [to_row(first, k) for k in (1, 2, 3)], [], ("value", "packed", "kept"))
    pieces = onward(1, x1, packed)
    pieces, kept = after((pieces, kept))
    carried = products(0, (3, 4), kept)
    x2, packed, mixed12, kept = solve(1, pieces, [x1], ("value", "packed", "mixed", "kept"))
    pieces = onward(2, x2, packed)
    mixed12 = spread_x(mixed12, 0)
    carried = to_column(carried, 0, 2)
    pieces, kept = after((pieces, kept))
    p41 = products(1, (4,), kept)
    x3, packed = solve(2, pieces, [carried], ("value", "packed"))
    pieces = onward(3, x3, packed)
    p41 = to_column(p41, 1, 3)
    x4, mixed34 = solve(3, pieces, [x3, p41], ("value", "mixed"))
    mixed34 = spread_x(mixed34, 1)

    mixed34 = pick(column(1, 0, 0), table, mixed34[0], mixed34[1:])
    mixed12 = pick(column(0, 0, 0), table, mixed12[0], mixed12[1:])
    mixed12, mixed34 = after((mixed12, mixed34))
    spread34 = spread_y(mixed34)
    spread12 = spread_y(mixed12)
    spreads = spread12 + spread34
    mine = call(
        functools.partial(merge_kernel, levels), "merged", two, [SMEM] + [VMEM] * len(spreads), (table, *spreads)
    )
    out = call(
        final_kernel, "final", jax.ShapeDtypeStruct((levels, size, samples), F32), [SMEM] + [VMEM] * 3,
        (table, first, mine, other_core(mine)),
    )
    return base_solution, out[:, None]


def solution(mesh):
    placed = (
        P(AXES, None, None),
        P(AXES, None, None),
        P(None, "row", None, None),
        P(None, "row", None, None),
        P(None, AXES, None, None),
        P(None, AXES),
        P(None, AXES),
    )
    return jax.shard_map(
        on_device,
        mesh=mesh,
        in_specs=placed,
        out_specs=(P(AXES, None, None), P(None, "row", None, None)),
        check_vma=False,
    )
```

```python
import functools

import jax
import jax.numpy as jnp
from jax import lax
from jax.experimental import pallas as pl
from jax.experimental.pallas import tpu as pltpu
from jax.sharding import PartitionSpec as P

BF16, F32 = jnp.bfloat16, jnp.float32
AXES = ("col", "row")
NX = NY = NZ = 4
BOTH = (0, 1)
SMEM = pl.BlockSpec(memory_space=pltpu.SMEM)
VMEM = pl.BlockSpec(memory_space=pltpu.VMEM)
HBM = pl.BlockSpec(memory_space=pltpu.HBM)


def column(x, y, core):
    return (y * NX + x) * 2 + core


def place(x, y, core, z):
    return column(x, y, core) * NZ + z


def dot(a, b):
    return jnp.dot(a, b, preferred_element_type=F32)


def call(body, name, outs, in_specs, args, scratch=(), flops=0, nbytes=0, out_specs=None, aliases=None):
    return pl.pallas_call(
        body,
        out_shape=outs,
        in_specs=in_specs,
        out_specs=out_specs or jax.tree.map(lambda _: VMEM, outs),
        scratch_shapes=list(scratch),
        input_output_aliases=aliases or {},
        compiler_params=pltpu.CompilerParams(vmem_limit_bytes=24 * 1024 * 1024),
        cost_estimate=pl.CostEstimate(flops=flops, bytes_accessed=nbytes, transcendentals=0),
        name=name,
    )(*args)


def base_solve_kernel(inverse_ref, rhs_ref, out_ref, *rest):
    count = rhs_ref.shape[0]
    rounded_refs, (inverse, rhs, value, sems) = rest[:count], rest[count:]
    reads, writes = [], []
    for i in range(count):
        reads.append((
            pltpu.make_async_copy(inverse_ref.at[i], inverse.at[i], sems.at[0, i]),
            pltpu.make_async_copy(rhs_ref.at[i], rhs.at[i], sems.at[1, i]),
        ))
        for copy in reads[-1]:
            copy.start()
    for i in range(count):
        for copy in reads[i]:
            copy.wait()
        value[i] = dot(inverse[i], rhs[i].astype(BF16))
        writes.append(pltpu.make_async_copy(value.at[i], out_ref.at[i], sems.at[2, i]))
        writes[-1].start()
        rounded_refs[i][...] = value[i].astype(BF16)
    for copy in writes:
        copy.wait()


def add_products(total, level, slots, low, high, operand_of, table, held_ref, copy_of=None):
    for slot in range(slots):
        source = table[level, slot]

        @pl.when(slot < table[level, slots])
        def _():
            if copy_of is not None:
                copy_of(level, slot).wait()

            @pl.when((source >= low) & (source < high))
            def _():
                total[...] += dot(held_ref[level * slots + slot], operand_of(source - low))


def base_kernel(levels, slots, table, factor_ref, inverse_ref, *rest):
    pieces, (keep_ref, send_ref, held_ref, kept_ref, operands, total, sems, other_sem) = rest[:-8], rest[-8:]

    def copy_of(level, slot):
        at = level * slots + slot
        return pltpu.make_async_copy(factor_ref.at[level, slot], held_ref.at[at], sems.at[at])

    for level in range(levels):
        for slot in range(slots):
            @pl.when(slot < table[level, slots])
            def _():
                copy_of(level, slot).start()
    inverses = pltpu.make_async_copy(inverse_ref, kept_ref, other_sem)
    inverses.start()
    row, core = table[levels, 0], table[levels, 1]
    per_row = len(pieces) // NZ
    for k in range(NZ):
        for i in range(per_row):
            operands[lax.rem(row + NZ - k, NZ) * per_row + i] = pieces[k * per_row + i][...]
    shares, some = keep_ref.shape[0], keep_ref.shape[1] // levels
    mine = pl.multiple_of(core * shares * some, shares * some)
    other = pl.multiple_of((1 - core) * shares * some, shares * some)
    for level in range(levels):
        total[...] = jnp.zeros_like(total)
        add_products(total, level, slots, 0, NZ * per_row, lambda q: operands[q], table, held_ref, copy_of)
        for share in range(shares):
            place_in = pl.ds(level * some, some)
            keep_ref[share, place_in] = total[pl.ds(mine + share * some, some)]
            send_ref[share, place_in] = total[pl.ds(other + share * some, some)].astype(BF16)
    inverses.wait()


def first_kernel(table, half_ref, other_ref, apex_ref, inverse_ref, ahead_ref, out_ref, target):
    levels = apex_ref.shape[0]
    core = table[levels, 1]
    shares, some = half_ref.shape[0], half_ref.shape[1] // levels
    for level in range(levels):
        to = target if level == 0 else ahead_ref.at[level - 1]
        for ref, side in ((half_ref, core), (other_ref, 1 - core)):
            for share in range(shares):
                rows = pl.ds(pl.multiple_of(side * shares * some, shares * some) + share * some, some)
                to[rows] = apex_ref[level, rows] - ref[share, pl.ds(level * some, some)].astype(F32)
        if level == 0:
            out_ref[...] = dot(inverse_ref[0], target[...].astype(BF16)).astype(BF16)


def sum_kernel(in_ref, out_ref):
    total = in_ref[0].astype(F32)
    for i in range(1, in_ref.shape[0]):
        total = total + in_ref[i].astype(F32)
    for i in range(in_ref.shape[0]):
        out_ref[i] = total.astype(BF16)


def solve_kernel(level, slots, low, extra, outs, table, held_ref, ahead_ref, inverse_ref,
                 *rest):
    pieces, more, outs_refs = rest[:NZ], rest[NZ : NZ + extra], rest[NZ + extra : NZ + extra + len(outs)]
    operands, total = rest[NZ + extra + len(outs) :]
    named = dict(zip(outs, outs_refs))
    nearest = pieces[0]
    chained = len(nearest.shape) == 3
    row = table[inverse_ref.shape[0], 0]
    operands[row] = nearest[0] if chained else nearest[...]
    for k in range(1, NZ):
        operands[lax.rem(row + NZ - k, NZ)] = pieces[k][...]
    lists = (table, held_ref)
    total[...] = nearest[1].astype(F32) if chained else jnp.zeros_like(total)
    for ref in more[1 if "mixed" in named else 0 :]:
        total[...] += (ref[0] if len(ref.shape) == 3 else ref[...]).astype(F32)
    add_products(total, level, slots, low, low + NZ, lambda q: operands[q], *lists)
    correction = (ahead_ref[level - 1] - total[...]).astype(BF16)
    value = dot(inverse_ref[level], correction).astype(BF16)
    named["value"][...] = value
    if "packed" in named:
        named["packed"][0] = value
        carried = [ref for ref in more if len(ref.shape) == 3]
        total[...] = carried[0][1].astype(F32) if carried else jnp.zeros_like(total)
        add_products(total, level + 1, slots, low, low + NZ, lambda q: operands[q], *lists)
        named["packed"][1] = total[...].astype(BF16)
    if "mixed" in named:
        named["mixed"][...] = jnp.where(table[inverse_ref.shape[0], 1] == 0, more[0][...], value)
    if "kept" in named:
        for v in range(NZ):
            named["kept"][v] = operands[v]


def later_kernel(levels, slots, low, table, held_ref, operands, out_ref, total):
    for i, level in enumerate(levels):
        total[...] = jnp.zeros_like(total)
        add_products(total, level, slots, low, low + NZ, lambda q: operands[q], table, held_ref)
        out_ref[i] = total[...].astype(BF16)


def pair_kernel(keep_ref, got_ref, out_ref):
    out_ref[...] = (keep_ref[...] + got_ref[...].astype(F32)).astype(BF16)


def pick_kernel(levels, column_of, table, value_ref, *rest):
    got, out_ref = rest[:-1], rest[-1]
    came = got[0][...]
    for ref in got[1:]:
        came = came + ref[...]
    out_ref[...] = jnp.where(table[levels, 2] // 2 == column_of // 2, value_ref[...], came)


def merge_kernel(levels, table, *rest):
    refs, out_ref = rest[:-1], rest[-1]
    each = len(refs) // out_ref.shape[0]
    for i in range(out_ref.shape[0]):
        value, *got = refs[i * each : (i + 1) * each]
        came = got[0][...]
        for ref in got[1:]:
            came = came + ref[...]
        out_ref[i] = jnp.where(table[levels, 2] < 2 * NX, value[...], came)


def output_kernel(start, levels, table, *rest):
    refs, (out_ref, value, sem) = rest[:-3], rest[-3:]
    mine_ref, other_ref = refs[-2:]
    core = table[levels, 1]
    count = value.shape[0]
    if count == 3:
        value[0] = refs[0][...].astype(F32)
    for side in BOTH:
        value[count - 2 + side] = jnp.where(core == side, mine_ref[0], other_ref[0]).astype(F32)
    copy = pltpu.make_async_copy(value, out_ref.at[pl.ds(start, count)], sem)
    copy.start()
    copy.wait()


def rest_kernel(levels, table, out_before, mine_ref, other_ref, out_ref, value, sem):
    output_kernel(levels - 2, levels, table, mine_ref, other_ref, out_ref, value, sem)


def pick(column_of, table, value, got):
    return call(
        functools.partial(pick_kernel, table.shape[0] - 1, column_of), "picked", jax.ShapeDtypeStruct(value.shape, value.dtype),
        [SMEM] + [VMEM] * (1 + len(got)), (table, value, *got),
    )


def send(value, pairs):
    return lax.ppermute(value, AXES, pairs)


def to_column(value, sender, receiver, k=0):
    return send(value, [(sender * NZ + z, receiver * NZ + (z + k) % NZ) for z in range(NZ)])


def to_row(value, step):
    return lax.ppermute(value, "row", [(z, (z + step) % NZ) for z in range(NZ)])


def other_core(value):
    return lax.ppermute(value, "col", [(c, c ^ 1) for c in range(NX * NY * 2)])


def over_plane(value):
    groups = [[column(x, y, core) for y in range(NY) for x in range(NX)] for core in BOTH]
    return lax.all_to_all(value, "col", 0, 0, axis_index_groups=groups, tiled=True)


def spread_x(value, x0):
    return [value] + [
        send(value, [(place(x0, 0, core, z), place((x0 + dx) % NX, 0, core, z)) for core in BOTH for z in range(NZ)])
        for dx in (1, 3, 2)
    ]


def spread_y(value):
    got = [
        send(value, [
            (place(x, 0, core, z), place(x, y, core, z)) for x in range(NX) for core in BOTH for z in range(NZ)
        ])
        for y in (1, 3, 2)
    ]
    return [value] + got


def on_device(base_rhs, base_inverse, apex, top_inverse, factor_blocks, block_source, block_count):
    levels, slots = block_source.shape[0], factor_blocks.shape[1]
    per_row, size, samples = base_rhs.shape
    shares = NX * NY
    some = size // 2 // shares
    block = factor_blocks.shape[2:]
    here, row = lax.axis_index("col"), lax.axis_index("row")
    core = here % 2
    table = jnp.concatenate([block_source, block_count], axis=1)
    table = jnp.concatenate([table, jnp.pad(jnp.stack([row, core, here]), (0, slots - 2))[None].astype(jnp.int32)])
    after = lax.optimization_barrier
    in_hbm = functools.partial(pltpu.with_memory_space_constraint, memory_space=pltpu.HBM)
    one = 2 * size * size * samples
    full = jax.ShapeDtypeStruct((size, samples), BF16)

    base_solution, *rounded = call(
        base_solve_kernel, "base_solve", (jax.ShapeDtypeStruct(base_rhs.shape, F32),) + (full,) * per_row,
        [HBM, HBM], (in_hbm(base_inverse), in_hbm(base_rhs)), flops=per_row * one,
        nbytes=6 * base_rhs.size + 2 * base_inverse.size,
        scratch=[
            pltpu.VMEM(base_inverse.shape, BF16), pltpu.VMEM(base_rhs.shape, F32), pltpu.VMEM(base_rhs.shape, F32),
            pltpu.SemaphoreType.DMA((3, per_row)),
        ],
        out_specs=(HBM,) + (VMEM,) * per_row,
    )
    near = [to_row(rounded[0], 1), to_row(rounded[1], -1)]
    near += [to_row(rounded[1], 1), to_row(rounded[0], -1)]
    far = [to_row(near[0], 1), to_row(near[1], -1)]
    pieces = rounded + [near[0], near[2]] + far + [near[3], near[1]]
    keep, give, held, inverses = call(
        functools.partial(base_kernel, levels, slots), "base_products",
        (
            jax.ShapeDtypeStruct((shares, levels * some, samples), F32),
            jax.ShapeDtypeStruct((shares, levels * some, samples), BF16),
            pltpu.VMEM((levels * slots,) + block, BF16),
            pltpu.VMEM((levels,) + block, BF16),
        ),
        [SMEM, HBM, HBM] + [VMEM] * len(pieces), (table, factor_blocks, in_hbm(top_inverse[:, 0]), *pieces),
        scratch=[
            pltpu.VMEM((NZ * per_row, size, samples), BF16), pltpu.VMEM((size, samples), F32),
            pltpu.SemaphoreType.DMA((levels * slots,)), pltpu.SemaphoreType.DMA,
        ],
        flops=levels * slots * one // 2, nbytes=2 * factor_blocks.size,
    )
    held, inverses = (pltpu.with_memory_space_constraint(x, pltpu.VMEM) for x in (held, inverses))
    lists = (table, held)
    pair = call(
        pair_kernel, "pair_sums", jax.ShapeDtypeStruct(give.shape, BF16), [VMEM] * 2, (keep, other_core(give))
    )
    share = call(sum_kernel, "sum_shares", jax.ShapeDtypeStruct(pair.shape, BF16), [VMEM], (over_plane(pair),))
    half = over_plane(share)
    other = other_core(half)
    ahead, first = call(
        first_kernel, "solve_0", (jax.ShapeDtypeStruct((levels - 1, size, samples), F32), full),
        [SMEM] + [VMEM] * 4, (table, half, other, apex[:, 0], inverses),
        scratch=[pltpu.VMEM((size, samples), F32)], flops=one,
    )
    two = jax.ShapeDtypeStruct((2, size, samples), BF16)
    four = jax.ShapeDtypeStruct((NZ, size, samples), BF16)
    acc = pltpu.VMEM((size, samples), F32)

    def low(u):
        return per_row * NZ + u * NZ

    def solve(u, pieces, extra, outs):
        shapes = {"value": full, "packed": two, "mixed": full, "kept": four}
        return call(
            functools.partial(solve_kernel, u + 1, slots, low(u), len(extra), outs), f"solve_{u + 1}",
            tuple(shapes[o] for o in outs), [SMEM] + [VMEM] * (3 + NZ + len(extra)),
            (*lists, ahead, inverses, *pieces, *extra),
            scratch=[pltpu.VMEM(four.shape, BF16), acc], flops=5 * one,
        )

    def products(u, levels_made, kept):
        return call(
            functools.partial(later_kernel, levels_made, slots, low(u)), f"later_{u}",
            jax.ShapeDtypeStruct((len(levels_made), size, samples), BF16), [SMEM] + [VMEM] * 2, (*lists, kept),
            scratch=[acc], flops=4 * len(levels_made) * one,
        )

    def onward(u, value, packed):
        return [to_column(packed, u - 1, u)] + [to_column(value, u - 1, u, k) for k in (1, 2, 3)]

    x1, packed, kept = solve(0, [first] + [to_row(first, k) for k in (1, 2, 3)], [], ("value", "packed", "kept"))
    pieces = onward(1, x1, packed)
    pieces, kept = after((pieces, kept))
    carried = products(0, (3, 4), kept)
    x2, packed, mixed12, kept = solve(1, pieces, [x1], ("value", "packed", "mixed", "kept"))
    pieces = onward(2, x2, packed)
    mixed12 = spread_x(mixed12, 0)
    mixed12 = pick(column(0, 0, 0), table, mixed12[0], mixed12[1:])
    carried = to_column(carried, 0, 2)
    pieces, kept = after((pieces, kept))
    p41 = products(1, (4,), kept)
    x3, packed = solve(2, pieces, [carried], ("value", "packed"))
    pieces = onward(3, x3, packed)
    spread12 = spread_y(after((mixed12, x3))[0])
    p41 = to_column(p41, 1, 3)
    x4, mixed34 = solve(3, pieces, [x3, p41], ("value", "mixed"))
    mixed34 = spread_x(mixed34, 1)
    spread34 = spread_y(pick(column(1, 0, 0), table, mixed34[0], mixed34[1:]))
    def merged(spread, name):
        single = jax.ShapeDtypeStruct((1, size, samples), BF16)
        value = call(
            functools.partial(merge_kernel, levels), name, single, [SMEM] + [VMEM] * len(spread), (table, *spread)
        )
        return value, other_core(value)

    shape = jax.ShapeDtypeStruct((levels, size, samples), F32)
    out = call(
        functools.partial(output_kernel, 0, levels), "output_first", shape, [SMEM] + [VMEM] * 3,
        (table, first, *merged(spread12, "merged_first")), out_specs=HBM,
        scratch=[pltpu.VMEM((3, size, samples), F32), pltpu.SemaphoreType.DMA],
    )
    out = call(
        functools.partial(rest_kernel, levels), "output_rest", shape, [SMEM, HBM] + [VMEM] * 2,
        (table, out, *merged(spread34, "merged_rest")), out_specs=HBM, aliases={1: 0},
        scratch=[pltpu.VMEM((2, size, samples), F32), pltpu.SemaphoreType.DMA],
    )
    return base_solution, out[:, None]


def solution(mesh):
    placed = (
        P(AXES, None, None),
        P(AXES, None, None),
        P(None, "row", None, None),
        P(None, "row", None, None),
        P(None, AXES, None, None),
        P(None, AXES),
        P(None, AXES),
    )
    return jax.shard_map(
        on_device,
        mesh=mesh,
        in_specs=placed,
        out_specs=(P(AXES, None, None), P(None, "row", None, None)),
        check_vma=False,
    )
```

```python
import functools

import jax
import jax.numpy as jnp
from jax import lax
from jax.experimental import pallas as pl
from jax.experimental.pallas import tpu as pltpu
from jax.sharding import PartitionSpec as P

BF16, F32 = jnp.bfloat16, jnp.float32
AXES = ("col", "row")
NX = NY = NZ = 4
BOTH = (0, 1)
SMEM = pl.BlockSpec(memory_space=pltpu.SMEM)
VMEM = pl.BlockSpec(memory_space=pltpu.VMEM)
HBM = pl.BlockSpec(memory_space=pltpu.HBM)


def column(x, y, core):
    return (y * NX + x) * 2 + core


def place(x, y, core, z):
    return column(x, y, core) * NZ + z


def dot(a, b):
    return jnp.dot(a, b, preferred_element_type=F32)


def call(body, name, outs, in_specs, args, scratch=(), flops=0, nbytes=0, out_specs=None, aliases=None):
    return pl.pallas_call(
        body,
        out_shape=outs,
        in_specs=in_specs,
        out_specs=out_specs or jax.tree.map(lambda _: VMEM, outs),
        scratch_shapes=list(scratch),
        input_output_aliases=aliases or {},
        compiler_params=pltpu.CompilerParams(vmem_limit_bytes=24 * 1024 * 1024),
        cost_estimate=pl.CostEstimate(flops=flops, bytes_accessed=nbytes, transcendentals=0),
        name=name,
    )(*args)


def base_solve_kernel(inverse_ref, rhs_ref, out_ref, *rest):
    count = rhs_ref.shape[0]
    rounded_refs, (inverse, rhs, value, sems) = rest[:count], rest[count:]
    reads, writes = [], []
    for i in range(count):
        reads.append((
            pltpu.make_async_copy(inverse_ref.at[i], inverse.at[i], sems.at[0, i]),
            pltpu.make_async_copy(rhs_ref.at[i], rhs.at[i], sems.at[1, i]),
        ))
        for copy in reads[-1]:
            copy.start()
    for i in range(count):
        for copy in reads[i]:
            copy.wait()
        value[i] = dot(inverse[i], rhs[i].astype(BF16))
        writes.append(pltpu.make_async_copy(value.at[i], out_ref.at[i], sems.at[2, i]))
        writes[-1].start()
        rounded_refs[i][...] = value[i].astype(BF16)
    for copy in writes:
        copy.wait()


def add_products(total, level, slots, low, high, operand_of, table, held_ref, copy_of=None):
    for slot in range(slots):
        source = table[level, slot]

        @pl.when(slot < table[level, slots])
        def _():
            if copy_of is not None:
                copy_of(level, slot).wait()

            @pl.when((source >= low) & (source < high))
            def _():
                total[...] += dot(held_ref[level * slots + slot], operand_of(source - low))


def base_kernel(levels, slots, table, factor_ref, inverse_ref, *rest):
    pieces, (keep_ref, send_ref, held_ref, kept_ref, operands, total, sems, other_sem) = rest[:-8], rest[-8:]

    def copy_of(level, slot):
        at = level * slots + slot
        return pltpu.make_async_copy(factor_ref.at[level, slot], held_ref.at[at], sems.at[at])

    for level in range(levels):
        for slot in range(slots):
            @pl.when(slot < table[level, slots])
            def _():
                copy_of(level, slot).start()
    inverses = pltpu.make_async_copy(inverse_ref, kept_ref, other_sem)
    inverses.start()
    row, core = table[levels, 0], table[levels, 1]
    per_row = len(pieces) // NZ
    for k in range(NZ):
        for i in range(per_row):
            operands[lax.rem(row + NZ - k, NZ) * per_row + i] = pieces[k * per_row + i][...]
    shares, some = keep_ref.shape[0], keep_ref.shape[1] // levels
    mine = pl.multiple_of(core * shares * some, shares * some)
    other = pl.multiple_of((1 - core) * shares * some, shares * some)
    for level in range(levels):
        total[...] = jnp.zeros_like(total)
        add_products(total, level, slots, 0, NZ * per_row, lambda q: operands[q], table, held_ref, copy_of)
        for share in range(shares):
            place_in = pl.ds(level * some, some)
            keep_ref[share, place_in] = total[pl.ds(mine + share * some, some)]
            send_ref[share, place_in] = total[pl.ds(other + share * some, some)].astype(BF16)
    inverses.wait()


def first_kernel(table, half_ref, other_ref, apex_ref, inverse_ref, ahead_ref, out_ref, target):
    levels = apex_ref.shape[0]
    core = table[levels, 1]
    shares, some = half_ref.shape[0], half_ref.shape[1] // levels
    for level in range(levels):
        to = target if level == 0 else ahead_ref.at[level - 1]
        for ref, side in ((half_ref, core), (other_ref, 1 - core)):
            for share in range(shares):
                rows = pl.ds(pl.multiple_of(side * shares * some, shares * some) + share * some, some)
                to[rows] = apex_ref[level, rows] - ref[share, pl.ds(level * some, some)].astype(F32)
        if level == 0:
            out_ref[...] = dot(inverse_ref[0], target[...].astype(BF16)).astype(BF16)


def sum_kernel(in_ref, out_ref):
    total = in_ref[0].astype(F32)
    for i in range(1, in_ref.shape[0]):
        total = total + in_ref[i].astype(F32)
    for i in range(in_ref.shape[0]):
        out_ref[i] = total.astype(BF16)


def solve_kernel(level, slots, low, extra, outs, table, held_ref, ahead_ref, inverse_ref,
                 *rest):
    pieces, more, outs_refs = rest[:NZ], rest[NZ : NZ + extra], rest[NZ + extra : NZ + extra + len(outs)]
    operands, total = rest[NZ + extra + len(outs) :]
    named = dict(zip(outs, outs_refs))
    nearest = pieces[0]
    chained = len(nearest.shape) == 3
    row = table[inverse_ref.shape[0], 0]
    operands[row] = nearest[0] if chained else nearest[...]
    for k in range(1, NZ):
        operands[lax.rem(row + NZ - k, NZ)] = pieces[k][...]
    lists = (table, held_ref)
    total[...] = nearest[1].astype(F32) if chained else jnp.zeros_like(total)
    for ref in more[1 if "mixed" in named else 0 :]:
        total[...] += (ref[0] if len(ref.shape) == 3 else ref[...]).astype(F32)
    add_products(total, level, slots, low, low + NZ, lambda q: operands[q], *lists)
    correction = (ahead_ref[level - 1] - total[...]).astype(BF16)
    value = dot(inverse_ref[level], correction).astype(BF16)
    named["value"][...] = value
    if "packed" in named:
        named["packed"][0] = value
        carried = [ref for ref in more if len(ref.shape) == 3]
        total[...] = carried[0][1].astype(F32) if carried else jnp.zeros_like(total)
        add_products(total, level + 1, slots, low, low + NZ, lambda q: operands[q], *lists)
        named["packed"][1] = total[...].astype(BF16)
    if "mixed" in named:
        named["mixed"][...] = jnp.where(table[inverse_ref.shape[0], 1] == 0, more[0][...], value)
    if "kept" in named:
        for v in range(NZ):
            named["kept"][v] = operands[v]


def later_kernel(levels, slots, low, table, held_ref, operands, out_ref, total):
    for i, level in enumerate(levels):
        total[...] = jnp.zeros_like(total)
        add_products(total, level, slots, low, low + NZ, lambda q: operands[q], table, held_ref)
        out_ref[i] = total[...].astype(BF16)


def pair_kernel(keep_ref, got_ref, out_ref):
    out_ref[...] = (keep_ref[...] + got_ref[...].astype(F32)).astype(BF16)


def pick_kernel(levels, column_of, table, value_ref, *rest):
    got, out_ref = rest[:-1], rest[-1]
    came = got[0][...]
    for ref in got[1:]:
        came = came + ref[...]
    out_ref[...] = jnp.where(table[levels, 2] // 2 == column_of // 2, value_ref[...], came)


def merge_kernel(levels, table, *rest):
    refs, out_ref = rest[:-1], rest[-1]
    each = len(refs) // out_ref.shape[0]
    for i in range(out_ref.shape[0]):
        value, *got = refs[i * each : (i + 1) * each]
        came = got[0][...]
        for ref in got[1:]:
            came = came + ref[...]
        out_ref[i] = jnp.where(table[levels, 2] < 2 * NX, value[...], came)


def output_kernel(start, levels, table, *rest):
    refs, (out_ref, value, sem) = rest[:-3], rest[-3:]
    mine_ref, other_ref = refs[-2:]
    core = table[levels, 1]
    count = value.shape[0]
    if count == 3:
        value[0] = refs[0][...].astype(F32)
    for side in BOTH:
        value[count - 2 + side] = jnp.where(core == side, mine_ref[0], other_ref[0]).astype(F32)
    copy = pltpu.make_async_copy(value, out_ref.at[pl.ds(start, count)], sem)
    copy.start()
    copy.wait()


def rest_kernel(levels, table, out_before, mine_ref, other_ref, out_ref, value, sem):
    output_kernel(levels - 2, levels, table, mine_ref, other_ref, out_ref, value, sem)


def pick(column_of, table, value, got):
    return call(
        functools.partial(pick_kernel, table.shape[0] - 1, column_of), "picked", jax.ShapeDtypeStruct(value.shape, value.dtype),
        [SMEM] + [VMEM] * (1 + len(got)), (table, value, *got),
    )


def send(value, pairs):
    return lax.ppermute(value, AXES, pairs)


def to_column(value, sender, receiver, k=0):
    return send(value, [(sender * NZ + z, receiver * NZ + (z + k) % NZ) for z in range(NZ)])


def to_row(value, step):
    return lax.ppermute(value, "row", [(z, (z + step) % NZ) for z in range(NZ)])


def other_core(value):
    return lax.ppermute(value, "col", [(c, c ^ 1) for c in range(NX * NY * 2)])


def over_plane(value):
    groups = [[column(x, y, core) for y in range(NY) for x in range(NX)] for core in BOTH]
    return lax.all_to_all(value, "col", 0, 0, axis_index_groups=groups, tiled=True)


def spread_x(value, x0):
    return [value] + [
        send(value, [(place(x0, 0, core, z), place((x0 + dx) % NX, 0, core, z)) for core in BOTH for z in range(NZ)])
        for dx in (1, 3, 2)
    ]


def spread_y(value):
    got = [
        send(value, [
            (place(x, 0, core, z), place(x, y, core, z)) for x in range(NX) for core in BOTH for z in range(NZ)
        ])
        for y in (1, 3, 2)
    ]
    return [value] + got


def on_device(base_rhs, base_inverse, apex, top_inverse, factor_blocks, block_source, block_count):
    levels, slots = block_source.shape[0], factor_blocks.shape[1]
    per_row, size, samples = base_rhs.shape
    shares = NX * NY
    some = size // 2 // shares
    block = factor_blocks.shape[2:]
    here, row = lax.axis_index("col"), lax.axis_index("row")
    core = here % 2
    table = jnp.concatenate([block_source, block_count], axis=1)
    table = jnp.concatenate([table, jnp.pad(jnp.stack([row, core, here]), (0, slots - 2))[None].astype(jnp.int32)])
    after = lax.optimization_barrier
    in_hbm = functools.partial(pltpu.with_memory_space_constraint, memory_space=pltpu.HBM)
    one = 2 * size * size * samples
    full = jax.ShapeDtypeStruct((size, samples), BF16)

    base_solution, *rounded = call(
        base_solve_kernel, "base_solve", (jax.ShapeDtypeStruct(base_rhs.shape, F32),) + (full,) * per_row,
        [HBM, HBM], (in_hbm(base_inverse), in_hbm(base_rhs)), flops=per_row * one,
        nbytes=6 * base_rhs.size + 2 * base_inverse.size,
        scratch=[
            pltpu.VMEM(base_inverse.shape, BF16), pltpu.VMEM(base_rhs.shape, F32), pltpu.VMEM(base_rhs.shape, F32),
            pltpu.SemaphoreType.DMA((3, per_row)),
        ],
        out_specs=(HBM,) + (VMEM,) * per_row,
    )
    near = [to_row(rounded[0], 1), to_row(rounded[1], -1)]
    near += [to_row(rounded[1], 1), to_row(rounded[0], -1)]
    far = [to_row(near[0], 1), to_row(near[1], -1)]
    pieces = rounded + [near[0], near[2]] + far + [near[3], near[1]]
    keep, give, held, inverses = call(
        functools.partial(base_kernel, levels, slots), "base_products",
        (
            jax.ShapeDtypeStruct((shares, levels * some, samples), F32),
            jax.ShapeDtypeStruct((shares, levels * some, samples), BF16),
            pltpu.VMEM((levels * slots,) + block, BF16),
            pltpu.VMEM((levels,) + block, BF16),
        ),
        [SMEM, HBM, HBM] + [VMEM] * len(pieces), (table, factor_blocks, in_hbm(top_inverse[:, 0]), *pieces),
        scratch=[
            pltpu.VMEM((NZ * per_row, size, samples), BF16), pltpu.VMEM((size, samples), F32),
            pltpu.SemaphoreType.DMA((levels * slots,)), pltpu.SemaphoreType.DMA,
        ],
        flops=levels * slots * one // 2, nbytes=2 * factor_blocks.size,
    )
    held, inverses = (pltpu.with_memory_space_constraint(x, pltpu.VMEM) for x in (held, inverses))
    lists = (table, held)
    pair = call(
        pair_kernel, "pair_sums", jax.ShapeDtypeStruct(give.shape, BF16), [VMEM] * 2, (keep, other_core(give))
    )
    share = call(sum_kernel, "sum_shares", jax.ShapeDtypeStruct(pair.shape, BF16), [VMEM], (over_plane(pair),))
    half = over_plane(share)
    other = other_core(half)
    ahead, first = call(
        first_kernel, "solve_0", (jax.ShapeDtypeStruct((levels - 1, size, samples), F32), full),
        [SMEM] + [VMEM] * 4, (table, half, other, apex[:, 0], inverses),
        scratch=[pltpu.VMEM((size, samples), F32)], flops=one,
    )
    two = jax.ShapeDtypeStruct((2, size, samples), BF16)
    four = jax.ShapeDtypeStruct((NZ, size, samples), BF16)
    acc = pltpu.VMEM((size, samples), F32)

    def low(u):
        return per_row * NZ + u * NZ

    def solve(u, pieces, extra, outs):
        shapes = {"value": full, "packed": two, "mixed": full, "kept": four}
        return call(
            functools.partial(solve_kernel, u + 1, slots, low(u), len(extra), outs), f"solve_{u + 1}",
            tuple(shapes[o] for o in outs), [SMEM] + [VMEM] * (3 + NZ + len(extra)),
            (*lists, ahead, inverses, *pieces, *extra),
            scratch=[pltpu.VMEM(four.shape, BF16), acc], flops=5 * one,
        )

    def products(u, levels_made, kept):
        return call(
            functools.partial(later_kernel, levels_made, slots, low(u)), f"later_{u}",
            jax.ShapeDtypeStruct((len(levels_made), size, samples), BF16), [SMEM] + [VMEM] * 2, (*lists, kept),
            scratch=[acc], flops=4 * len(levels_made) * one,
        )

    def onward(u, value, packed):
        return [to_column(packed, u - 1, u)] + [to_column(value, u - 1, u, k) for k in (1, 2, 3)]

    after_one, before_one, across = (to_row(first, k) for k in (1, 3, 2))
    x1, packed, kept = solve(0, [first, after_one, across, before_one], [], ("value", "packed", "kept"))
    pieces = onward(1, x1, packed)
    pieces, kept = after((pieces, kept))
    carried = products(0, (3, 4), kept)
    x2, packed, mixed12, kept = solve(1, pieces, [x1], ("value", "packed", "mixed", "kept"))
    pieces = onward(2, x2, packed)
    mixed12 = spread_x(mixed12, 0)
    mixed12 = pick(column(0, 0, 0), table, mixed12[0], mixed12[1:])
    carried = to_column(carried, 0, 2)
    pieces, kept = after((pieces, kept))
    p41 = products(1, (4,), kept)
    x3, packed = solve(2, pieces, [carried], ("value", "packed"))
    pieces = onward(3, x3, packed)
    spread12 = spread_y(after((mixed12, x3))[0])
    p41 = to_column(p41, 1, 3)
    x4, mixed34 = solve(3, pieces, [x3, p41], ("value", "mixed"))
    mixed34 = spread_x(mixed34, 1)
    spread34 = spread_y(pick(column(1, 0, 0), table, mixed34[0], mixed34[1:]))
    def merged(spread, name):
        single = jax.ShapeDtypeStruct((1, size, samples), BF16)
        value = call(
            functools.partial(merge_kernel, levels), name, single, [SMEM] + [VMEM] * len(spread), (table, *spread)
        )
        return value, other_core(value)

    shape = jax.ShapeDtypeStruct((levels, size, samples), F32)
    out = call(
        functools.partial(output_kernel, 0, levels), "output_first", shape, [SMEM] + [VMEM] * 3,
        (table, first, *merged(spread12, "merged_first")), out_specs=HBM,
        scratch=[pltpu.VMEM((3, size, samples), F32), pltpu.SemaphoreType.DMA],
    )
    out = call(
        functools.partial(rest_kernel, levels), "output_rest", shape, [SMEM, HBM] + [VMEM] * 2,
        (table, out, *merged(spread34, "merged_rest")), out_specs=HBM, aliases={1: 0},
        scratch=[pltpu.VMEM((2, size, samples), F32), pltpu.SemaphoreType.DMA],
    )
    return base_solution, out[:, None]


def solution(mesh):
    placed = (
        P(AXES, None, None),
        P(AXES, None, None),
        P(None, "row", None, None),
        P(None, "row", None, None),
        P(None, AXES, None, None),
        P(None, AXES),
        P(None, AXES),
    )
    return jax.shard_map(
        on_device,
        mesh=mesh,
        in_specs=placed,
        out_specs=(P(AXES, None, None), P(None, "row", None, None)),
        check_vma=False,
    )
```
